32 devices in a mesh: groups: 2 (over x), store: 16 (over z, y, core).
Axes of the slice: x: 2, y: 2, z: 4, core: 2. Of those that a mesh axis runs over, the one named last changes fastest.
Arguments:
- activations: bfloat16 [8192, 4096], P(('groups', 'store')), parts along dimension 0, may hold values from -6 to 6
- out_grads: bfloat16 [8192, 14336], P(('groups', 'store')), parts along dimension 0, may hold values from -6 to 6
- basis_in: bfloat16 [32, 4096], replicated, may hold values from -0.09375 to 0.09375
- basis_out: bfloat16 [32, 14336], replicated, may hold values from -0.046875 to 0.046875
- lengths: int32 [32, 8], P(('groups', 'store')), parts along dimension 0, may hold values from 1 to 64, 256 in all within a row
- codes: int32 [131072, 1024], P(('groups', 'store')), parts along dimension 0, may hold values from -127 to 127
- scale_index: int32 [131072], P(('groups', 'store')), parts along dimension 0, may hold values from 68 to 131
- queries: bfloat16 [128, 1024], P(('groups', 'store')), parts along dimension 0, may hold values from -1.25 to 1.25
Outputs:
- new_rows: float32 [256, 1024], P(('groups', 'store')), parts along dimension 0
- store_scores: float32 [128, 65536], P('groups', 'store'), parts along dimension 0
- new_scores: float32 [128, 128], P('groups', 'store'), parts along dimension 0
The draws below stay inside these ranges and needn't reach their ends.
There are 2 independent parts, one for each index of `groups`. The reference program is written for one: setup_inputs(seed, part) draws one part's arguments, and reference() takes and returns one part's arrays. A program takes and returns all parts, laid end to end along the dimension named above; an argument that names none is the same for every part. Nothing has to cross between parts.
Inputs may be any that keep to these rules, and one draw needn't show every extreme that they name: Each row of lengths sums to 256.
All inputs are finite; a program needn't handle non-finite values.
Results may differ from the reference program's by a relative error of at most 0.0068.
Values may be sent and summed in bfloat16 or wider, within the bound.
No kernel may reach another device: no remote copies, remote signals or barrier semaphores. Data moves between devices by JAX's collectives and lax.ppermute only.
A program may use at most 128 MiB of HBM per device.

```python
import math
import jax
import jax.numpy as jnp
import numpy as np
from jax import lax

D_IN = 4096
D_OUT = 14336
RANK = 32
PROJ = 1024
TOK_DEV = 256
MOST = 64
EX_DEV = 8
ROWS_DEV = 4096
QUERIES = 64
TOKENS = 4096
EXAMPLES = 128
STORE_ROWS = 65536
N_STORE = 16


def draw_codes(key, part):
    key = jax.random.fold_in(key, 11)
    key_columns, key_first, key_second, key_values = jax.random.split(key, 4)
    levels_table = np.array([max(1, math.isqrt(1764 // (level + 1))) for level in range(PROJ)], dtype=np.int32)
    column_order = jax.random.permutation(key_columns, PROJ)
    amplitude = jnp.asarray(levels_table)[column_order][None, :]
    raw_values = jax.random.randint(key_values, (STORE_ROWS, PROJ), 0, 1048576)
    base_values = raw_values % (2 * amplitude + 1) - amplitude
    first_map = jax.random.permutation(key_first, PROJ)
    second_map = jax.random.permutation(key_second, PROJ)
    mixed = base_values + base_values[:, first_map] + base_values[:, second_map]
    mixed = mixed.reshape(N_STORE, ROWS_DEV, PROJ)
    row_index = jnp.arange(ROWS_DEV, dtype=jnp.int32)[None, :, None]
    column_index = jnp.arange(PROJ, dtype=jnp.int32)[None, None, :]
    mixed = jnp.where((row_index == 0) & (column_index == 0), 127, mixed)
    mixed = jnp.where((row_index == 1) & (column_index == 0), -127, mixed)
    return mixed.reshape(STORE_ROWS, PROJ).astype(jnp.int32)


def draw_scale_index(key, part):
    key = jax.random.fold_in(key, 7)
    base_draw = jax.random.randint(key, (N_STORE, ROWS_DEV), 0, 32)
    device = jnp.arange(N_STORE, dtype=jnp.int32)[:, None]
    offset = 32 * device // max(N_STORE - 1, 1)
    column = jnp.arange(ROWS_DEV, dtype=jnp.int32)[None, :]
    base_draw = jnp.where(column == 0, 31, jnp.where(column == 1, 0, base_draw))
    return (base_draw + offset + 68).reshape(-1).astype(jnp.int32)


def steps_of(rng, extent, cuts, smallest, high):
    def one(dim, shards_of):
        heights = jax.random.uniform(jax.random.fold_in(jax.random.fold_in(rng, 6), dim), (shards_of,), jnp.float32, smallest / len(cuts), high / len(cuts))
        return jnp.repeat(jnp.exp(heights), extent[dim] // shards_of).reshape((-1,) + (1,) * (len(extent) - dim - 1))

    loudness = one(*cuts[0])
    for cut in cuts[1:]:
        loudness = loudness * one(*cut)
    return loudness


def length_profile(number_of, total, limit, lean):
    weights = [(1 << 20) // math.isqrt(rank ** lean) + 1 for rank in range(2, number_of + 1)]
    spare, holding = total - limit - (number_of - 1), [1] * (number_of - 1)
    while spare > 0:
        candidates = [i for i in range(number_of - 1) if holding[i] < limit]
        pool, remaining = sum([weights[i] for i in candidates]), spare
        for i in candidates:
            addition = min(limit - holding[i], max(1, remaining * weights[i] // pool), spare)
            holding[i] = holding[i] + addition
            spare = spare - addition
    return np.array([limit] + holding)


def ragged(rng, number_of, total, reach, skew):
    if number_of == 2:
        one = jax.random.randint(rng, (), max(1, total - reach), min(reach, total - 1) + 1)
        return jnp.stack([one, total - one])
    sizes = jnp.asarray(length_profile(number_of, total, reach, skew), jnp.int32)
    couples = (number_of - 1) // 2
    donor, receiver = sizes[1:1 + 2 * couples:2], sizes[2:2 + 2 * couples:2]
    margin = jnp.minimum(donor - 1, reach - receiver)
    shifted = jax.random.randint(jax.random.fold_in(rng, 1), (couples,), 0, 1 << 20) % (margin + 1)
    sizes = sizes.at[1:1 + 2 * couples:2].set(donor - shifted).at[2:2 + 2 * couples:2].set(receiver + shifted)
    return sizes[jax.random.permutation(jax.random.fold_in(rng, 2), number_of)]


def gaussian(rng, dims, spread, reach, cuts=(), kind=jnp.bfloat16):
    factor_of = steps_of(rng, dims, cuts, -0.22, 0.18) if cuts else 1.0
    values = jax.random.normal(rng, dims, jnp.float32) * spread * factor_of
    return jnp.minimum(jnp.maximum(values, -reach), reach).astype(kind)


def setup_inputs(seed: int = 0, part: int = 0) -> dict:
    arg_keys = jax.random.split(jax.random.key(seed), 9)
    part_splits = jax.random.split(jax.random.fold_in(arg_keys[8], part), 9)
    activations = gaussian(part_splits[0], (TOKENS, D_IN), 1.0, 6.0, ((0, 16),))
    out_grads = gaussian(part_splits[1], (TOKENS, D_OUT), 1.0, 6.0, ((0, 16),))
    basis_in = gaussian(arg_keys[2], (RANK, D_IN), D_IN ** -0.5, 0.09375)
    basis_out = gaussian(arg_keys[3], (RANK, D_OUT), D_OUT ** -0.5, 0.046875)
    lengths = jax.vmap(lambda own: ragged(own, EX_DEV, TOK_DEV, MOST, 1))(jax.random.split(part_splits[4], N_STORE)).reshape((N_STORE, EX_DEV)).astype(jnp.int32)
    codes = draw_codes(jax.random.fold_in(jax.random.fold_in(arg_keys[8], part), 71), part)
    scale_index = draw_scale_index(jax.random.fold_in(jax.random.fold_in(arg_keys[8], part), 71), part)
    queries = gaussian(part_splits[7], (QUERIES, PROJ), 0.2, 1.25, ((0, 16),))
    return dict(activations=activations, out_grads=out_grads, basis_in=basis_in, basis_out=basis_out, lengths=lengths, codes=codes, scale_index=scale_index, queries=queries)


def reference(activations, out_grads, basis_in, basis_out, lengths, codes, scale_index, queries):
    highest = lax.Precision.HIGHEST
    proj_in = jnp.dot(activations.astype(jnp.float32), basis_in.T.astype(jnp.float32), preferred_element_type=jnp.float32)
    proj_out = jnp.dot(out_grads.astype(jnp.float32), basis_out.T.astype(jnp.float32), preferred_element_type=jnp.float32)
    proj_in = proj_in.reshape(N_STORE, TOK_DEV, RANK)
    proj_out = proj_out.reshape(N_STORE, TOK_DEV, RANK)
    finishes = jnp.cumsum(lengths, axis=1).astype(jnp.int32)
    starts = (finishes - lengths).astype(jnp.int32)
    position = jnp.arange(TOK_DEV, dtype=jnp.int32)[None, None, :]
    member = ((position >= starts[:, :, None]) & (position < finishes[:, :, None])).astype(jnp.float32)
    summed = jnp.einsum('net,nti,ntj->neij', member, proj_in, proj_out, precision=highest)
    new_rows = summed.reshape(EXAMPLES, PROJ)
    scales = jnp.exp2(scale_index.astype(jnp.float32) / 16.0) / 128.0
    stored = (codes.astype(jnp.float32) * scales[:, None]).astype(jnp.bfloat16)
    fisher = 0.75 / STORE_ROWS * jnp.dot(stored.T.astype(jnp.float32), stored.astype(jnp.float32), preferred_element_type=jnp.float32)
    fisher = fisher + 0.25 / EXAMPLES * jnp.dot(new_rows.T, new_rows, precision=highest)
    damping = 0.1 * jnp.trace(fisher) / PROJ
    system = fisher + damping * jnp.eye(PROJ, dtype=jnp.float32)
    factor = jnp.linalg.cholesky(system)
    right_side = queries.astype(jnp.float32).T
    middle = lax.linalg.triangular_solve(factor, right_side, left_side=True, lower=True)
    solved = lax.linalg.triangular_solve(factor, middle, left_side=True, lower=True, transpose_a=True)
    precond = solved.T
    store_scores = jnp.dot(precond, stored.astype(jnp.float32).T, precision=highest)
    new_scores = jnp.dot(precond, new_rows.T, precision=highest)
    return (new_rows, store_scores, new_scores)
```

```python
import functools

import jax
import jax.numpy as jnp
import numpy as np
from jax import lax
from jax.experimental import pallas as pl
from jax.experimental.pallas import tpu as pltpu
from jax.sharding import PartitionSpec as P

LANES = 128
PACK = 16
CODE_MAX = 32767.0
F32 = jnp.float32
BF16 = jnp.bfloat16
VMEM = pl.BlockSpec(memory_space=pltpu.VMEM)
SMEM = pl.BlockSpec(memory_space=pltpu.SMEM)
ANY = pl.BlockSpec(memory_space=pl.ANY)
NN = (((1,), (0,)), ((), ()))
NT = (((1,), (1,)), ((), ()))
TN = (((0,), (0,)), ((), ()))


def mm(left, right, dims=NN):
    return lax.dot_general(left, right, dims, preferred_element_type=F32)


def split2(value):
    high = value.astype(BF16)
    return high, (value - high.astype(F32)).astype(BF16)


def split3(value):
    high, _ = split2(value)
    rest = value - high.astype(F32)
    mid, low = split2(rest)
    return high, mid, low


def mm3(left, right, dims=NN):
    left_high, left_low = left
    right_high, right_low = right
    return mm(left_high, right_high, dims) + (
        mm(left_high, right_low, dims) + mm(left_low, right_high, dims)
    )


def triangle(width):
    tiles = width // LANES
    return [(i, j) for i in range(tiles) for j in range(i + 1)]


def column_of(row):
    return jnp.broadcast_to(row, (LANES, LANES)).T


def eye(size):
    return lax.broadcasted_iota(jnp.int32, (size, size), 0) == lax.broadcasted_iota(
        jnp.int32, (size, size), 1
    )


def gram_kernel(
    steps,
    weight_store,
    weight_new,
    me_ref,
    lengths_ref,
    codes_ref,
    scale_ref,
    act_ref,
    grad_ref,
    basis_in_ref,
    basis_out_ref,
    stored_ref,
    new_rows_ref,
    keep_ref,
    send_ref,
    diag_ref,
    total,
    proj_in,
    proj_out,
):
    step = pl.program_id(0)
    chunk, width = codes_ref.shape
    rank = basis_in_ref.shape[0]
    tokens = act_ref.shape[0]
    examples = new_rows_ref.shape[0]

    @pl.when(step == 0)
    def _():
        total[...] = jnp.zeros_like(total)
        proj_in[...] = jnp.zeros_like(proj_in)
        proj_out[...] = jnp.zeros_like(proj_out)

    groups = chunk // LANES
    for g in range(groups):
        index = scale_ref[pl.ds(step * groups + g, 1), :]
        scale = column_of(jnp.exp2(index.astype(F32) / 16.0) / 128.0)
        rows = slice(g * LANES, (g + 1) * LANES)
        for c in range(width // LANES):
            cols = slice(c * LANES, (c + 1) * LANES)
            stored_ref[rows, cols] = (codes_ref[rows, cols].astype(F32) * scale).astype(BF16)
    stored = stored_ref[...]
    side = 256
    for i in range(width // side):
        rows = slice(i * side, (i + 1) * side)
        total[rows, : (i + 1) * side] += mm(stored[:, rows], stored[:, : (i + 1) * side], TN)
    proj_in[...] += mm(act_ref[...], basis_in_ref[...], NT)
    proj_out[...] += mm(grad_ref[...], basis_out_ref[...], NT)

    @pl.when(step == steps - 1)
    def _():
        wide = (3 * rank, width)
        k = lax.broadcasted_iota(jnp.int32, wide, 0) % rank
        c = lax.broadcasted_iota(jnp.int32, wide, 1)
        pick_in = (k == c // rank).astype(F32).astype(BF16)
        pick_out = (k == c % rank).astype(F32).astype(BF16)
        left = mm(jnp.concatenate(split3(proj_in[...]), axis=1), pick_in)
        right = mm(jnp.concatenate(split3(proj_out[...]), axis=1), pick_out)
        products = split3(left * right)
        place = lax.broadcasted_iota(jnp.int32, (examples, tokens), 1)
        owner = lax.broadcasted_iota(jnp.int32, (examples, tokens), 0)
        member = jnp.zeros((examples, tokens), F32)
        start = jnp.int32(0)
        for e in range(examples):
            finish = start + lengths_ref[0, e]
            inside = (owner == e) & (place >= start) & (place < finish)
            member = jnp.where(inside, 1.0, member)
            start = finish
        member = member.astype(BF16)
        new_rows = mm(member, products[0]) + (mm(member, products[1]) + mm(member, products[2]))
        new_rows_ref[...] = new_rows
        high, mid, low = [part.astype(F32) for part in split3(new_rows)]
        first = jnp.concatenate([high, high, mid, high, low, mid], axis=0).astype(BF16)
        second = jnp.concatenate([high, mid, high, low, high, mid], axis=0).astype(BF16)
        for i in range(width // side):
            rows = slice(i * side, (i + 1) * side)
            total[rows, : (i + 1) * side] = weight_store * total[
                rows, : (i + 1) * side
            ] + weight_new * mm(first[:, rows], second[:, : (i + 1) * side], TN)
        tiles = triangle(width)
        half = len(tiles) // 2
        diagonal = eye(LANES)
        for i in range(width // LANES):
            at = slice(i * LANES, (i + 1) * LANES)
            diag_ref[i : i + 1, :] = jnp.sum(
                jnp.where(diagonal, total[at, at], 0.0), axis=0, keepdims=True
            )
        send_ref[half * LANES :, :] = diag_ref[...]
        for b, (i, j) in enumerate(tiles):
            rows = slice(b % half * LANES, (b % half + 1) * LANES)
            tile = total[i * LANES : (i + 1) * LANES, j * LANES : (j + 1) * LANES]

            @pl.when(me_ref[0] == b // half)
            def _():
                keep_ref[rows, :] = tile

            @pl.when(me_ref[0] != b // half)
            def _():
                send_ref[rows, :] = tile


def gram(me, lengths, codes, scale_index, activations, out_grads, basis_in, basis_out, count):
    rows, width = codes.shape
    tokens, inputs = activations.shape
    outputs = out_grads.shape[1]
    rank = basis_in.shape[0]
    examples = lengths.shape[1]
    steps = 8
    half = len(triangle(width)) // 2 * LANES
    chunk = rows // steps
    whole = lambda *shape: pl.BlockSpec(shape, lambda s: (0,) * len(shape))
    return pl.pallas_call(
        functools.partial(
            gram_kernel, steps, 0.75 / (count * rows), 0.25 / (count * examples)
        ),
        grid=(steps,),
        in_specs=[
            SMEM,
            SMEM,
            pl.BlockSpec((chunk, width), lambda s: (s, 0)),
            whole(rows // LANES, LANES),
            pl.BlockSpec((tokens, inputs // steps), lambda s: (0, s)),
            pl.BlockSpec((tokens, outputs // steps), lambda s: (0, s)),
            pl.BlockSpec((rank, inputs // steps), lambda s: (0, s)),
            pl.BlockSpec((rank, outputs // steps), lambda s: (0, s)),
        ],
        out_specs=[
            pl.BlockSpec((chunk, width), lambda s: (s, 0)),
            whole(examples, width),
            whole(half, LANES),
            whole(half + width // LANES, LANES),
            whole(width // LANES, LANES),
        ],
        out_shape=[
            jax.ShapeDtypeStruct((rows, width), BF16),
            jax.ShapeDtypeStruct((examples, width), F32),
            jax.ShapeDtypeStruct((half, LANES), F32),
            jax.ShapeDtypeStruct((half + width // LANES, LANES), F32),
            jax.ShapeDtypeStruct((width // LANES, LANES), F32),
        ],
        scratch_shapes=[
            pltpu.VMEM((width, width), F32),
            pltpu.VMEM((tokens, rank), F32),
            pltpu.VMEM((tokens, rank), F32),
        ],
        compiler_params=pltpu.CompilerParams(vmem_limit_bytes=48 << 20),
        cost_estimate=pl.CostEstimate(
            flops=6 * 10**9, bytes_accessed=40 * 10**6, transcendentals=0
        ),
        name="fisher_share",
    )(me, lengths, codes, scale_index, activations, out_grads, basis_in, basis_out)


def exponents(diag):
    return jnp.clip(jnp.ceil(32.0 * jnp.log2(jnp.maximum(diag, 1e-30))), -4000.0, 4000.0)


def fill_scales(exps, factor, columns, rows_ref):
    scale = jnp.exp2(exps / 64.0)
    rows_ref[...] = scale * factor
    for t in range(exps.shape[0]):
        columns[t * LANES : (t + 1) * LANES, :] = column_of(scale[t : t + 1, :])


def read_exps(ref, start, tiles):
    return ref[start : start + PACK, :].astype(jnp.int32).astype(F32)[:tiles, :]


def write_exps(ref, start, exps):
    tiles = exps.shape[0]
    padded = jnp.concatenate([exps, jnp.zeros((PACK - tiles, LANES), F32)], axis=0)
    ref[start : start + PACK, :] = padded.astype(jnp.int32).astype(jnp.int16)


def encode(value, inverse):
    scaled = jnp.clip(jnp.round(value * inverse), -CODE_MAX, CODE_MAX)
    return scaled.astype(jnp.int32).astype(jnp.int16)


def strip_scale(table_ref, columns, rows_ref, flat, strip):
    tile = flat // LANES
    i = table_ref[0, tile]
    j = table_ref[1, tile]
    at = pl.multiple_of(i * LANES + flat % LANES, strip)
    return columns[pl.ds(at, strip), :] * rows_ref[pl.ds(j, 1), :]


def combine_kernel(members, coded, tiles, strip, *refs):
    where_ref, table_ref, own_ref, state_ref = refs[:4]
    arrived = refs[4 : 4 + coded]
    refs = refs[4 + coded :]
    out_own, out_state = refs[:2]
    out_messages = refs[2 : 1 + members] if members > 1 else ()
    refs = refs[max(1, members) + 1 :]
    columns, rows_ref, inverse_columns, inverse_rows = refs
    rows = own_ref.shape[0]
    if coded == 1 and arrived[0].dtype == F32:
        exps = exponents(state_ref[...] + arrived[0][rows:, :])
    else:
        mine = read_exps(state_ref, 0, tiles)
        theirs = [read_exps(ref, rows, tiles) for ref in arrived]
        level = [jnp.exp2(e / 32.0) for e in [mine] + theirs]
        while len(level) > 1:
            level = [a + b for a, b in zip(level[::2], level[1::2])]
        exps = exponents(level[0])
        for m, e in enumerate(theirs):
            fill_scales(e, 1.0 / CODE_MAX, columns.at[m], rows_ref.at[m])
    fill_scales(-exps, CODE_MAX, inverse_columns, inverse_rows)
    base = where_ref[0]
    mine_at = where_ref[1]
    part = rows // max(members, 1)
    for m in range(max(members, 1)):
        first = jnp.bitwise_xor(mine_at, m) * part

        def body(s, _):
            inside = pl.multiple_of(s * strip, strip)
            at = pl.multiple_of(first + inside, strip)
            flat = base + at
            value = own_ref[pl.ds(at, strip), :]
            for a, ref in enumerate(arrived):
                got = ref[pl.ds(at, strip), :]
                if got.dtype == F32:
                    value = value + got
                else:
                    got = got.astype(jnp.int32).astype(F32)
                    value = value + got * strip_scale(
                        table_ref, columns.at[a], rows_ref.at[a], flat, strip
                    )
            if members > 1 and m == 0:
                out_own[pl.ds(inside, strip), :] = value
            else:
                inverse = strip_scale(table_ref, inverse_columns, inverse_rows, flat, strip)
                target = out_messages[m - 1] if members > 1 else out_own
                target[pl.ds(inside, strip), :] = encode(value, inverse)
            return 0

        lax.fori_loop(0, part // strip, body, 0, unroll=2)
    write_exps(out_state, 0, exps)
    for ref in out_messages:
        write_exps(ref, part, exps)


def combine(where, table, own, state, arrived, members, strip):
    rows = own.shape[0]
    tiles = table.shape[1]
    width_tiles = int(round(((8 * tiles + 1) ** 0.5 - 1) / 2))
    width = width_tiles * LANES
    part = rows // max(members, 1)
    outs = [
        jax.ShapeDtypeStruct((part, LANES), F32 if members > 1 else jnp.int16),
        jax.ShapeDtypeStruct((PACK, LANES), jnp.int16),
    ]
    outs += [jax.ShapeDtypeStruct((part + PACK, LANES), jnp.int16)] * max(members - 1, 0)
    return pl.pallas_call(
        functools.partial(combine_kernel, members, len(arrived), width_tiles, strip),
        in_specs=[SMEM, SMEM] + [VMEM] * (2 + len(arrived)),
        out_specs=[VMEM] * len(outs),
        out_shape=outs,
        scratch_shapes=[
            pltpu.VMEM((len(arrived), width, LANES), F32),
            pltpu.VMEM((len(arrived), width_tiles, LANES), F32),
            pltpu.VMEM((width, LANES), F32),
            pltpu.VMEM((width_tiles, LANES), F32),
        ],
        compiler_params=pltpu.CompilerParams(vmem_limit_bytes=32 << 20),
        cost_estimate=pl.CostEstimate(
            flops=10 * rows * LANES, bytes_accessed=8 * rows * LANES, transcendentals=0
        ),
        name="sum_shares",
    )(where, table, own, state, *arrived)


def solve_kernel(
    side,
    places_ref,
    first_ref,
    second_ref,
    state_ref,
    queries_ref,
    new_rows_ref,
    stored_hbm,
    scores_ref,
    new_scores_ref,
    flat,
    system,
    pair,
    stored,
    solved,
    columns,
    rows_ref,
    sem,
):
    copy = pltpu.make_async_copy(stored_hbm, stored, sem)
    copy.start()
    queries, width = queries_ref.shape
    tiles = width // LANES
    pieces = places_ref.shape[0]
    piece = flat.shape[0] // pieces
    for p in range(pieces):
        source = first_ref if p < pieces // 2 else second_ref
        at = p % (pieces // 2) * piece
        flat[pl.ds(pl.multiple_of(places_ref[p], PACK), piece), :] = source[at : at + piece, :]
    fill_scales(read_exps(state_ref, 0, tiles), 1.0 / CODE_MAX, columns, rows_ref)
    diagonal = eye(LANES)
    trace = jnp.zeros((1, LANES), F32)
    for b, (i, j) in enumerate(triangle(width)):
        value = flat[b * LANES : (b + 1) * LANES, :].astype(jnp.int32).astype(F32)
        value = value * columns[i * LANES : (i + 1) * LANES, :] * rows_ref[j : j + 1, :]
        system[i * LANES : (i + 1) * LANES, j * LANES : (j + 1) * LANES] = value
        if i == j:
            trace = trace + jnp.sum(jnp.where(diagonal, value, 0.0), axis=0, keepdims=True)
        elif i * LANES // side == j * LANES // side:
            system[j * LANES : (j + 1) * LANES, i * LANES : (i + 1) * LANES] = value.T
    damp = (0.1 / width) * jnp.sum(trace)
    for i in range(tiles):
        at = slice(i * LANES, (i + 1) * LANES)
        system[at, at] += jnp.where(diagonal, damp, 0.0)
    system[width:, :] = queries_ref[...].astype(F32)
    blocks = width // side
    spans = [slice(b * side, (b + 1) * side) for b in range(blocks)]
    bounds = [
        jnp.max(jnp.sum(jnp.abs(system[span, span]), axis=0, keepdims=True)) for span in spans
    ]
    unit = eye(side)
    for b, span in enumerate(spans):
        below = (b + 1) * side
        bound = bounds[b]
        low = damp / bound
        pair[:side, :] = jnp.where(unit, 1.0 / bound, 0.0)
        pair[side:, :] = system[span, span] * (1.0 / bound)

        def more(low):
            return low < 0.9995

        def newton(low):
            gain = 4.0 / ((1.0 + low) * (1.0 + low))
            both = pair[...]
            step = jnp.where(unit, gain * (1.0 + low), 0.0) - gain * both[side:, :]
            pair[...] = mm3(split2(both), split2(step))
            return gain * low

        lax.while_loop(more, newton, low)
        inverse = split2(pair[:side, :])
        panel = system[below:, span]
        weights = split2(mm3(split2(panel), inverse))
        later = split2(panel[: width - below, :])
        system[below:, span] = weights[0].astype(F32) + weights[1].astype(F32)
        for c in range(b + 1, blocks):
            from_row = c * side - below
            update = mm3(
                (weights[0][from_row:, :], weights[1][from_row:, :]),
                (
                    later[0][from_row : from_row + side, :],
                    later[1][from_row : from_row + side, :],
                ),
                NT,
            )
            system[c * side :, spans[c]] -= update
    for b in reversed(range(blocks)):
        below = (b + 1) * side
        value = system[width:, spans[b]]
        if below < width:
            value = value - mm3(
                split2(solved[:, below:]), split2(system[below:width, spans[b]])
            )
        solved[:, spans[b]] = value
    high, low = split2(solved[...])
    new_scores_ref[...] = mm3((high, low), split2(new_rows_ref[...]), NT)
    both = jnp.concatenate([high, low], axis=0)
    copy.wait()
    span = 512
    for r in range(0, stored.shape[0], span):
        value = mm(both, stored[r : r + span, :], NT)
        scores_ref[:, r : r + span] = value[:queries, :] + value[queries:, :]


def solve(places, first, second, state, queries, new_rows, stored):
    count, width = queries.shape
    rows = stored.shape[0]
    examples = new_rows.shape[0]
    side = 256
    flat_rows = len(triangle(width)) * LANES
    return pl.pallas_call(
        functools.partial(solve_kernel, side),
        in_specs=[SMEM] + [VMEM] * 5 + [ANY],
        out_specs=[VMEM, VMEM],
        out_shape=[
            jax.ShapeDtypeStruct((count, rows), F32),
            jax.ShapeDtypeStruct((count, examples), F32),
        ],
        scratch_shapes=[
            pltpu.VMEM((flat_rows, LANES), jnp.int16),
            pltpu.VMEM((width + count, width), F32),
            pltpu.VMEM((2 * side, side), F32),
            pltpu.VMEM((rows, width), BF16),
            pltpu.VMEM((count, width), F32),
            pltpu.VMEM((width, LANES), F32),
            pltpu.VMEM((width // LANES, LANES), F32),
            pltpu.SemaphoreType.DMA,
        ],
        compiler_params=pltpu.CompilerParams(vmem_limit_bytes=48 << 20),
        cost_estimate=pl.CostEstimate(
            flops=10 * 10**9, bytes_accessed=20 * 10**6, transcendentals=0
        ),
        name="solve_and_score",
    )(places, first, second, state, queries, new_rows, stored)


def swap(value, mask, count):
    return lax.ppermute(value, "store", [(i, i ^ mask) for i in range(count)])


def shards(activations, out_grads, basis_in, basis_out, lengths, codes, scale_index, queries):
    count = lax.axis_size("store")
    me = lax.axis_index("store")
    width = codes.shape[1]
    tiles = triangle(width)
    table = np.array(tiles, np.int32).T
    all_queries = lax.all_gather(queries, "store", axis=0, tiled=True)
    core = me & 1
    stored, new_rows, own, send, state = gram(
        core.astype(jnp.int32)[None],
        lengths,
        codes,
        scale_index.reshape(-1, LANES),
        activations,
        out_grads,
        basis_in,
        basis_out,
        count,
    )
    groups = []
    bit = 1
    while 1 << bit < count:
        members = 4 if 1 << (bit + 1) < count else 2
        groups.append((bit, members))
        bit += 2
    piece = len(tiles) * LANES // count
    strip = int(np.gcd(np.gcd(piece, LANES), 64))
    arrived = [swap(send, 1, count)]
    base = core * own.shape[0]
    for bit, members in groups:
        at = (me >> bit) & (members - 1)
        where = jnp.stack([base, at]).astype(jnp.int32)
        own, state, *messages = combine(where, table, own, state, arrived, members, strip)
        arrived = [swap(message, (m + 1) << bit, count) for m, message in enumerate(messages)]
        base = base + at * own.shape[0]
    where = jnp.stack([base, jnp.zeros_like(base)]).astype(jnp.int32)
    final, state = combine(where, table, own, state, arrived, 0, strip)
    for bit, members in reversed(groups):
        final = jnp.concatenate(
            [final] + [swap(final, m << bit, count) for m in range(1, members)], axis=0
        )
    other = swap(final, 1, count)
    places = []
    for slot in range(count):
        size = len(tiles) * LANES // 2
        place = (core ^ (slot // (count // 2))) * size
        left = slot % (count // 2)
        weight = count // 2
        for bit, members in groups:
            weight //= members
            size //= members
            place = place + (((me >> bit) & (members - 1)) ^ (left // weight)) * size
            left %= weight
        places.append(place)
    scores, new_scores = solve(
        jnp.stack(places).astype(jnp.int32), final, other, state, all_queries, new_rows, stored
    )
    return new_rows, scores, new_scores


def solution(mesh):
    return jax.shard_map(
        shards,
        mesh=mesh,
        in_specs=(
            P(("groups", "store"), None),
            P(("groups", "store"), None),
            P(),
            P(),
            P(("groups", "store"), None),
            P(("groups", "store"), None),
            P(("groups", "store")),
            P(("groups", "store"), None),
        ),
        out_specs=(P(("groups", "store"), None), P("groups", "store"), P("groups", "store")),
        check_vma=False,
    )
```

```python
import functools

import jax
import jax.numpy as jnp
import numpy as np
from jax import lax
from jax.experimental import pallas as pl
from jax.experimental.pallas import tpu as pltpu
from jax.sharding import PartitionSpec as P

LANES = 128
PACK = 16
CODE_MAX = 32767.0
F32 = jnp.float32
BF16 = jnp.bfloat16
VMEM = pl.BlockSpec(memory_space=pltpu.VMEM)
SMEM = pl.BlockSpec(memory_space=pltpu.SMEM)
ANY = pl.BlockSpec(memory_space=pl.ANY)
NN = (((1,), (0,)), ((), ()))
NT = (((1,), (1,)), ((), ()))
TN = (((0,), (0,)), ((), ()))


def mm(left, right, dims=NN):
    return lax.dot_general(left, right, dims, preferred_element_type=F32)


def split2(value):
    high = value.astype(BF16)
    return high, (value - high.astype(F32)).astype(BF16)


def split3(value):
    high, _ = split2(value)
    rest = value - high.astype(F32)
    mid, low = split2(rest)
    return high, mid, low


def mm3(left, right, dims=NN):
    left_high, left_low = left
    right_high, right_low = right
    return mm(left_high, right_high, dims) + (
        mm(left_high, right_low, dims) + mm(left_low, right_high, dims)
    )


def triangle(width):
    tiles = width // LANES
    return [(i, j) for i in range(tiles) for j in range(i + 1)]


def column_of(row):
    return jnp.broadcast_to(row, (LANES, LANES)).T


def eye(size):
    return lax.broadcasted_iota(jnp.int32, (size, size), 0) == lax.broadcasted_iota(
        jnp.int32, (size, size), 1
    )


def code_floats(value):
    size = jnp.abs(value.astype(F32))
    power = jnp.floor(jnp.log2(jnp.maximum(size, 2.0**-126)))
    mantissa = size * jnp.exp2(-power)
    power = power + jnp.where(mantissa >= 2.0, 1.0, 0.0) - jnp.where(mantissa < 1.0, 1.0, 0.0)
    mantissa = jnp.where(
        mantissa >= 2.0, mantissa * 0.5, jnp.where(mantissa < 1.0, mantissa * 2.0, mantissa)
    )
    code = (power + 127.0) * 128.0 + jnp.round((mantissa - 1.0) * 128.0)
    code = jnp.where(size < 2.0**-126, 0.0, code)
    return jnp.where(value.astype(F32) < 0.0, -code, code)


def float_of(code):
    size = jnp.abs(code)
    power = lax.shift_right_logical(size, 7).astype(F32) - 127.0
    value = (1.0 + (size & 127).astype(F32) / 128.0) * jnp.exp2(power)
    value = jnp.where(size == 0, 0.0, value)
    return jnp.where(code < 0, -value, value)


def decode(codes_ref, scale_ref, start, target_ref):
    rows, width = target_ref.shape
    for g in range(rows // LANES):
        index = scale_ref[pl.ds(start // LANES + g, 1), :]
        scale = column_of(jnp.exp2(index.astype(F32) / 16.0) / 128.0)
        at = pl.multiple_of(start + g * LANES, LANES)
        for c in range(width // LANES):
            cols = slice(c * LANES, (c + 1) * LANES)
            value = codes_ref[pl.ds(at, LANES), cols].astype(F32) * scale
            target_ref[g * LANES : (g + 1) * LANES, cols] = value.astype(BF16)


def gram_kernel(
    weight_store,
    weight_new,
    me_ref,
    lengths_ref,
    scale_ref,
    queries_ref,
    act_hbm,
    grad_hbm,
    basis_in_hbm,
    basis_out_hbm,
    codes_hbm,
    new_rows_ref,
    keep_ref,
    send_ref,
    diag_ref,
    asked_ref,
    act,
    grad,
    basis_in,
    basis_out,
    codes,
    stored,
    stored_next,
    total,
    sems,
    code_sems,
):
    rows, width = codes.shape
    rank = basis_in.shape[0]
    tokens = act.shape[0]
    examples = new_rows_ref.shape[0]
    chunk = stored.shape[0]
    cuts = 4
    span = grad.shape[1] // cuts
    parts = [(basis_out_hbm, basis_out)]
    for c in range(cuts):
        at = (slice(None), slice(c * span, (c + 1) * span))
        parts.append((grad_hbm.at[at], grad.at[at]))
    parts += [(basis_in_hbm, basis_in), (act_hbm, act)]
    copies = [
        pltpu.make_async_copy(source, target, sems.at[i])
        for i, (source, target) in enumerate(parts)
    ]

    def code_copy(c):
        at = pl.ds(pl.multiple_of(c * chunk, chunk), chunk)
        return pltpu.make_async_copy(codes_hbm.at[at, :], codes.at[at, :], code_sems.at[c])

    chunks = rows // chunk
    for c in range(chunks // 2):
        code_copy(c).start()
    for copy in copies:
        copy.start()
    for c in range(chunks // 2, chunks):
        code_copy(c).start()
    asked = code_floats(queries_ref[...])
    asked = [asked[:, i * LANES : (i + 1) * LANES] for i in range(width // LANES)]
    asked_ref[...] = jnp.concatenate(asked, axis=0).astype(jnp.int32).astype(jnp.int16)
    side = 256

    def ready(c, target):
        code_copy(c).wait()
        decode(codes, scale_ref, c * chunk, target)

    def add(source, first):
        for i in range(width // side):
            at = slice(i * side, (i + 1) * side)
            to = slice(0, (i + 1) * side)
            value = mm(source[:, at], source[:, to], TN)
            total[at, to] = value if first else total[at, to] + value

    ready(0, stored)
    ready(1, stored_next)
    add(stored, True)

    def body(pair, _):
        ready(2 * pair + 2, stored)
        add(stored_next, False)
        ready(2 * pair + 3, stored_next)
        add(stored, False)
        return 0

    lax.fori_loop(0, chunks // 4 - 1, body, 0)
    copies[0].wait()
    proj_out = jnp.zeros((tokens, rank), F32)
    for c in range(cuts):
        copies[1 + c].wait()
        at = (slice(None), slice(c * span, (c + 1) * span))
        proj_out = proj_out + mm(grad[at], basis_out[at], NT)
    copies[-2].wait()
    copies[-1].wait()
    proj_in = mm(act[...], basis_in[...], NT)
    wide = (3 * rank, width)
    k = lax.broadcasted_iota(jnp.int32, wide, 0) & (rank - 1)
    c = lax.broadcasted_iota(jnp.int32, wide, 1)
    pick_in = (k == lax.shift_right_logical(c, rank.bit_length() - 1)).astype(F32).astype(BF16)
    pick_out = (k == (c & (rank - 1))).astype(F32).astype(BF16)
    left = mm(jnp.concatenate(split3(proj_in), axis=1), pick_in)
    right = mm(jnp.concatenate(split3(proj_out), axis=1), pick_out)
    products = split3(left * right)
    place = lax.broadcasted_iota(jnp.int32, (examples, tokens), 1)
    owner = lax.broadcasted_iota(jnp.int32, (examples, tokens), 0)
    member = jnp.zeros((examples, tokens), F32)
    start = jnp.int32(0)
    for e in range(examples):
        finish = start + lengths_ref[0, e]
        inside = (owner == e) & (place >= start) & (place < finish)
        member = jnp.where(inside, 1.0, member)
        start = finish
    member = member.astype(BF16)
    new_rows = mm(member, products[0]) + (mm(member, products[1]) + mm(member, products[2]))
    new_rows_ref[...] = new_rows
    high, mid, low = [part.astype(F32) for part in split3(new_rows)]
    first = jnp.concatenate([high, high, mid, high, low, mid], axis=0).astype(BF16)
    second = jnp.concatenate([high, mid, high, low, high, mid], axis=0).astype(BF16)
    lax.fori_loop(chunks // 4 - 1, chunks // 2 - 1, body, 0)
    add(stored_next, False)
    tiles = triangle(width)
    half = len(tiles) // 2
    diagonal = eye(LANES)

    def finish(mine):
        for i in range(width // side):
            for j in range(i + 1):
                down = slice(i * side, (i + 1) * side)
                across = slice(j * side, (j + 1) * side)
                value = weight_store * total[down, across] + weight_new * mm(
                    first[:, down], second[:, across], TN
                )
                for b, (p, q) in enumerate(tiles):
                    if p // 2 != i or q // 2 != j:
                        continue
                    tile = value[
                        p % 2 * LANES : (p % 2 + 1) * LANES, q % 2 * LANES : (q % 2 + 1) * LANES
                    ]
                    target = keep_ref if b // half == mine else send_ref
                    target[b % half * LANES : (b % half + 1) * LANES, :] = tile
                    if p == q:
                        diag_ref[p : p + 1, :] = jnp.sum(
                            jnp.where(diagonal, tile, 0.0), axis=0, keepdims=True
                        )

    for mine in range(2):
        pl.when(me_ref[0] == mine)(functools.partial(finish, mine))
    send_ref[half * LANES :, :] = diag_ref[...]


def gram(
    me, lengths, codes, scale_index, queries, activations, out_grads, basis_in, basis_out, count
):
    rows, width = codes.shape
    examples = lengths.shape[1]
    half = len(triangle(width)) // 2 * LANES
    chunk = 256
    extra = width // LANES
    return pl.pallas_call(
        functools.partial(gram_kernel, 0.75 / (count * rows), 0.25 / (count * examples)),
        in_specs=[SMEM, SMEM, VMEM, VMEM] + [ANY] * 5,
        out_specs=[VMEM] * 5,
        out_shape=[
            jax.ShapeDtypeStruct((examples, width), F32),
            jax.ShapeDtypeStruct((half, LANES), F32),
            jax.ShapeDtypeStruct((half + extra, LANES), F32),
            jax.ShapeDtypeStruct((extra, LANES), F32),
            jax.ShapeDtypeStruct((queries.shape[0] * extra, LANES), jnp.int16),
        ],
        scratch_shapes=[
            pltpu.VMEM(activations.shape, BF16),
            pltpu.VMEM(out_grads.shape, BF16),
            pltpu.VMEM(basis_in.shape, BF16),
            pltpu.VMEM(basis_out.shape, BF16),
            pltpu.VMEM((rows, width), jnp.int32),
            pltpu.VMEM((chunk, width), BF16),
            pltpu.VMEM((chunk, width), BF16),
            pltpu.VMEM((width, width), F32),
            pltpu.SemaphoreType.DMA((8,)),
            pltpu.SemaphoreType.DMA((rows // chunk,)),
        ],
        compiler_params=pltpu.CompilerParams(vmem_limit_bytes=60 << 20),
        cost_estimate=pl.CostEstimate(
            flops=6 * 10**9, bytes_accessed=30 * 10**6, transcendentals=0
        ),
        name="fisher_share",
    )(
        me,
        lengths,
        scale_index,
        queries,
        activations,
        out_grads,
        basis_in,
        basis_out,
        codes,
    )


def exponents(diag):
    return jnp.clip(jnp.ceil(32.0 * jnp.log2(jnp.maximum(diag, 1e-30))), -4000.0, 4000.0)


def fill_scales(exps, factor, columns, rows_ref):
    scale = jnp.exp2(exps / 64.0)
    rows_ref[...] = scale * factor
    for t in range(exps.shape[0]):
        columns[t * LANES : (t + 1) * LANES, :] = column_of(scale[t : t + 1, :])


def read_exps(ref, start, tiles):
    return ref[start : start + PACK, :].astype(jnp.int32).astype(F32)[:tiles, :]


def write_exps(ref, start, exps):
    tiles = exps.shape[0]
    padded = jnp.concatenate([exps, jnp.zeros((PACK - tiles, LANES), F32)], axis=0)
    ref[start : start + PACK, :] = padded.astype(jnp.int32).astype(jnp.int16)


def encode(value, inverse):
    scaled = jnp.clip(jnp.round(value * inverse), -CODE_MAX, CODE_MAX)
    return scaled.astype(jnp.int32).astype(jnp.int16)


def strip_scale(table_ref, columns, rows_ref, flat, strip):
    tile = flat // LANES
    i = table_ref[0, tile]
    j = table_ref[1, tile]
    at = pl.multiple_of(i * LANES + flat % LANES, strip)
    return columns[pl.ds(at, strip), :] * rows_ref[pl.ds(j, 1), :]


def combine_kernel(members, coded, tiles, strip, *refs):
    where_ref, table_ref, own_ref, state_ref = refs[:4]
    arrived = refs[4 : 4 + coded]
    refs = refs[4 + coded :]
    if not members:
        asked_ref, refs = refs[0], refs[1:]
    out_own, out_state = refs[:2]
    out_messages = refs[2 : 1 + members] if members > 1 else ()
    refs = refs[max(1, members) + 1 :]
    columns, rows_ref, inverse_columns, inverse_rows = refs
    rows = own_ref.shape[0]
    if coded == 1 and arrived[0].dtype == F32:
        exps = exponents(state_ref[...] + arrived[0][rows:, :])
    else:
        mine = read_exps(state_ref, 0, tiles)
        theirs = [read_exps(ref, rows, tiles) for ref in arrived]
        level = [jnp.exp2(e / 32.0) for e in [mine] + theirs]
        while len(level) > 1:
            level = [a + b for a, b in zip(level[::2], level[1::2])]
        exps = exponents(level[0])
        for m, e in enumerate(theirs):
            fill_scales(e, 1.0 / CODE_MAX, columns.at[m], rows_ref.at[m])
    fill_scales(-exps, CODE_MAX, inverse_columns, inverse_rows)
    base = where_ref[0]
    mine_at = where_ref[1]
    part = rows // max(members, 1)
    for m in range(max(members, 1)):
        first = jnp.bitwise_xor(mine_at, m) * part

        def body(s, _):
            inside = pl.multiple_of(s * strip, strip)
            at = pl.multiple_of(first + inside, strip)
            flat = base + at
            value = own_ref[pl.ds(at, strip), :]
            for a, ref in enumerate(arrived):
                got = ref[pl.ds(at, strip), :]
                if got.dtype == F32:
                    value = value + got
                else:
                    got = got.astype(jnp.int32).astype(F32)
                    value = value + got * strip_scale(
                        table_ref, columns.at[a], rows_ref.at[a], flat, strip
                    )
            if members > 1 and m == 0:
                out_own[pl.ds(inside, strip), :] = value
            else:
                inverse = strip_scale(table_ref, inverse_columns, inverse_rows, flat, strip)
                target = out_messages[m - 1] if members > 1 else out_own
                target[pl.ds(inside, strip), :] = encode(value, inverse)
            return 0

        lax.fori_loop(0, part // strip, body, 0, unroll=2)
    write_exps(out_state, 0, exps)
    if not members:
        out_own[rows:, :] = asked_ref[...]
    for ref in out_messages:
        write_exps(ref, part, exps)


def combine(where, table, own, state, arrived, members, strip, asked=()):
    rows = own.shape[0]
    tiles = table.shape[1]
    width_tiles = int(round(((8 * tiles + 1) ** 0.5 - 1) / 2))
    width = width_tiles * LANES
    part = rows // max(members, 1)
    outs = [
        jax.ShapeDtypeStruct(
            (part + sum(a.shape[0] for a in asked), LANES), F32 if members > 1 else jnp.int16
        ),
        jax.ShapeDtypeStruct((PACK, LANES), jnp.int16),
    ]
    outs += [jax.ShapeDtypeStruct((part + PACK, LANES), jnp.int16)] * max(members - 1, 0)
    return pl.pallas_call(
        functools.partial(combine_kernel, members, len(arrived), width_tiles, strip),
        in_specs=[SMEM, SMEM] + [VMEM] * (2 + len(arrived) + len(asked)),
        out_specs=[VMEM] * len(outs),
        out_shape=outs,
        scratch_shapes=[
            pltpu.VMEM((len(arrived), width, LANES), F32),
            pltpu.VMEM((len(arrived), width_tiles, LANES), F32),
            pltpu.VMEM((width, LANES), F32),
            pltpu.VMEM((width_tiles, LANES), F32),
        ],
        compiler_params=pltpu.CompilerParams(vmem_limit_bytes=32 << 20),
        cost_estimate=pl.CostEstimate(
            flops=10 * rows * LANES, bytes_accessed=8 * rows * LANES, transcendentals=0
        ),
        name="sum_shares",
    )(where, table, own, state, *arrived, *asked)


def solve_kernel(
    side,
    slot_bits,
    places_ref,
    first_ref,
    second_ref,
    state_ref,
    new_rows_ref,
    scale_ref,
    codes_hbm,
    scores_ref,
    new_scores_ref,
    flat,
    system,
    pair,
    stored,
    solved,
    columns,
    rows_ref,
    codes,
    sem,
):
    copy = pltpu.make_async_copy(codes_hbm, codes, sem)
    copy.start()
    queries, width = solved.shape
    tiles = width // LANES
    pieces = places_ref.shape[0] - 1
    piece = flat.shape[0] // pieces
    pitch = 2 * first_ref.shape[0] // pieces
    asked = []
    for p in range(pieces):
        source = first_ref if p < pieces // 2 else second_ref
        at = p % (pieces // 2) * pitch
        flat[pl.ds(pl.multiple_of(places_ref[p], PACK), piece), :] = source[at : at + piece, :]
        asked.append(source[at + piece : at + pitch, :].astype(jnp.int32))
    asked = float_of(jnp.concatenate(asked, axis=0)).astype(BF16)
    each = queries // pieces
    order = (tiles * queries, asked.shape[0])
    to = lax.broadcasted_iota(jnp.int32, order, 0)
    source = lax.broadcasted_iota(jnp.int32, order, 1)
    slot = lax.shift_right_logical(source, (pitch - piece).bit_length() - 1)
    owner = jnp.zeros(order, jnp.int32)
    for bit, position in enumerate(slot_bits):
        owner = owner | ((lax.shift_right_logical(slot, position) & 1) << bit)
    owner = owner ^ places_ref[pieces]
    inside = source & (pitch - piece - 1)
    target = (
        lax.shift_right_logical(inside, each.bit_length() - 1) * queries
        + owner * each
        + (inside & (each - 1))
    )
    asked = mm((target == to).astype(F32).astype(BF16), asked)
    for i in range(tiles):
        system[width:, i * LANES : (i + 1) * LANES] = asked[i * queries : (i + 1) * queries, :]
    fill_scales(read_exps(state_ref, 0, tiles), 1.0 / CODE_MAX, columns, rows_ref)
    diagonal = eye(LANES)
    trace = jnp.zeros((1, LANES), F32)
    for b, (i, j) in enumerate(triangle(width)):
        value = flat[b * LANES : (b + 1) * LANES, :].astype(jnp.int32).astype(F32)
        value = value * columns[i * LANES : (i + 1) * LANES, :] * rows_ref[j : j + 1, :]
        system[i * LANES : (i + 1) * LANES, j * LANES : (j + 1) * LANES] = value
        if i == j:
            trace = trace + jnp.sum(jnp.where(diagonal, value, 0.0), axis=0, keepdims=True)
        elif i * LANES // side == j * LANES // side:
            system[j * LANES : (j + 1) * LANES, i * LANES : (i + 1) * LANES] = value.T
    damp = (0.1 / width) * jnp.sum(trace)
    for i in range(tiles):
        at = slice(i * LANES, (i + 1) * LANES)
        system[at, at] += jnp.where(diagonal, damp, 0.0)
    blocks = width // side
    spans = [slice(b * side, (b + 1) * side) for b in range(blocks)]
    bounds = [
        jnp.max(jnp.sum(jnp.abs(system[span, span]), axis=0, keepdims=True)) for span in spans
    ]
    unit = eye(side)
    for b, span in enumerate(spans):
        below = (b + 1) * side
        bound = bounds[b]
        low = damp / bound
        pair[:side, :] = jnp.where(unit, 1.0 / bound, 0.0)
        pair[side:, :] = system[span, span] * (1.0 / bound)

        def more(low):
            return low < 0.9995

        def newton(low):
            gain = 4.0 / ((1.0 + low) * (1.0 + low))
            both = pair[...]
            step = jnp.where(unit, gain * (1.0 + low), 0.0) - gain * both[side:, :]
            pair[...] = mm3(split2(both), split2(step))
            return gain * low

        lax.while_loop(more, newton, low)
        inverse = split2(pair[:side, :])
        panel = system[below:, span]
        weights = split2(mm3(split2(panel), inverse))
        later = split2(panel[: width - below, :])
        system[below:, span] = weights[0].astype(F32) + weights[1].astype(F32)
        for c in range(b + 1, blocks):
            from_row = c * side - below
            update = mm3(
                (weights[0][from_row:, :], weights[1][from_row:, :]),
                (
                    later[0][from_row : from_row + side, :],
                    later[1][from_row : from_row + side, :],
                ),
                NT,
            )
            system[c * side :, spans[c]] -= update
    for b in reversed(range(blocks)):
        below = (b + 1) * side
        value = system[width:, spans[b]]
        if below < width:
            value = value - mm3(
                split2(solved[:, below:]), split2(system[below:width, spans[b]])
            )
        solved[:, spans[b]] = value
    high, low = split2(solved[...])
    new_scores_ref[...] = mm3((high, low), split2(new_rows_ref[...]), NT)
    both = jnp.concatenate([high, low], axis=0)
    copy.wait()
    span = stored.shape[0]

    def score(c, _):
        at = pl.multiple_of(c * span, span)
        decode(codes, scale_ref, at, stored)
        value = mm(both, stored[...], NT)
        scores_ref[:, pl.ds(at, span)] = value[:queries, :] + value[queries:, :]
        return 0

    lax.fori_loop(0, codes.shape[0] // span, score, 0, unroll=2)


def solve(places, slot_bits, first, second, state, new_rows, scale_index, codes, count):
    rows, width = codes.shape
    examples = new_rows.shape[0]
    side = 256
    span = 512
    flat_rows = len(triangle(width)) * LANES
    return pl.pallas_call(
        functools.partial(solve_kernel, side, slot_bits),
        in_specs=[SMEM] + [VMEM] * 5 + [ANY],
        out_specs=[VMEM, VMEM],
        out_shape=[
            jax.ShapeDtypeStruct((count, rows), F32),
            jax.ShapeDtypeStruct((count, examples), F32),
        ],
        scratch_shapes=[
            pltpu.VMEM((flat_rows, LANES), jnp.int16),
            pltpu.VMEM((width + count, width), F32),
            pltpu.VMEM((2 * side, side), F32),
            pltpu.VMEM((span, width), BF16),
            pltpu.VMEM((count, width), F32),
            pltpu.VMEM((width, LANES), F32),
            pltpu.VMEM((width // LANES, LANES), F32),
            pltpu.VMEM((rows, width), jnp.int32),
            pltpu.SemaphoreType.DMA,
        ],
        compiler_params=pltpu.CompilerParams(vmem_limit_bytes=60 << 20),
        cost_estimate=pl.CostEstimate(
            flops=10 * 10**9, bytes_accessed=20 * 10**6, transcendentals=0
        ),
        name="solve_and_score",
    )(places, first, second, state, new_rows, scale_index, codes)


def swap(value, mask, count):
    return lax.ppermute(value, "store", [(i, i ^ mask) for i in range(count)])


def shards(activations, out_grads, basis_in, basis_out, lengths, codes, scale_index, queries):
    count = lax.axis_size("store")
    me = lax.axis_index("store")
    width = codes.shape[1]
    tiles = triangle(width)
    table = np.array(tiles, np.int32).T
    core = me & 1
    scale_index = scale_index.reshape(-1, LANES)
    new_rows, own, send, state, asked = gram(
        core.astype(jnp.int32)[None],
        lengths,
        codes,
        scale_index,
        queries,
        activations,
        out_grads,
        basis_in,
        basis_out,
        count,
    )
    groups = []
    bit = 1
    while 1 << bit < count:
        members = 4 if 1 << (bit + 1) < count else 2
        groups.append((bit, members))
        bit += 2
    piece = len(tiles) * LANES // count
    strip = int(np.gcd(np.gcd(piece, LANES), 64))
    arrived = [swap(send, 1, count)]
    base = core * own.shape[0]
    for bit, members in groups:
        at = (me >> bit) & (members - 1)
        where = jnp.stack([base, at]).astype(jnp.int32)
        own, state, *messages = combine(where, table, own, state, arrived, members, strip)
        arrived = [swap(message, (m + 1) << bit, count) for m, message in enumerate(messages)]
        base = base + at * own.shape[0]
    where = jnp.stack([base, jnp.zeros_like(base)]).astype(jnp.int32)
    final, state = combine(where, table, own, state, arrived, 0, strip, [asked])
    for bit, members in reversed(groups):
        final = jnp.concatenate(
            [final] + [swap(final, m << bit, count) for m in range(1, members)], axis=0
        )
    other = swap(final, 1, count)
    slot_bits = [count.bit_length() - 2]
    for bit, members in groups:
        for low in range(members // 2):
            slot_bits.append(slot_bits[0] - (bit + members // 2 - 1) + low)
    places = []
    for slot in range(count):
        mask = sum((slot >> position & 1) << b for b, position in enumerate(slot_bits))
        owner = me ^ mask
        place = (owner & 1) * (len(tiles) * LANES // 2)
        size = len(tiles) * LANES // 2
        for bit, members in groups:
            size //= members
            place = place + ((owner >> bit) & (members - 1)) * size
        places.append(place)
    scores, new_scores = solve(
        jnp.stack(places + [me]).astype(jnp.int32),
        slot_bits,
        final,
        other,
        state,
        new_rows,
        scale_index,
        codes,
        count * queries.shape[0],
    )
    return new_rows, scores, new_scores


def solution(mesh):
    return jax.shard_map(
        shards,
        mesh=mesh,
        in_specs=(
            P(("groups", "store"), None),
            P(("groups", "store"), None),
            P(),
            P(),
            P(("groups", "store"), None),
            P(("groups", "store"), None),
            P(("groups", "store")),
            P(("groups", "store"), None),
        ),
        out_specs=(P(("groups", "store"), None), P("groups", "store"), P("groups", "store")),
        check_vma=False,
    )
```

```python
import functools

import jax
import jax.numpy as jnp
import numpy as np
from jax import lax
from jax.experimental import pallas as pl
from jax.experimental.pallas import tpu as pltpu
from jax.sharding import PartitionSpec as P

LANES = 128
PACK = 16
CODE_MAX = 32767.0
F32 = jnp.float32
BF16 = jnp.bfloat16
VMEM = pl.BlockSpec(memory_space=pltpu.VMEM)
SMEM = pl.BlockSpec(memory_space=pltpu.SMEM)
ANY = pl.BlockSpec(memory_space=pl.ANY)
NN = (((1,), (0,)), ((), ()))
NT = (((1,), (1,)), ((), ()))
TN = (((0,), (0,)), ((), ()))


def mm(left, right, dims=NN):
    return lax.dot_general(left, right, dims, preferred_element_type=F32)


def split2(value):
    high = value.astype(BF16)
    return high, (value - high.astype(F32)).astype(BF16)


def split3(value):
    high, _ = split2(value)
    rest = value - high.astype(F32)
    mid, low = split2(rest)
    return high, mid, low


def mm3(left, right, dims=NN):
    left_high, left_low = left
    right_high, right_low = right
    return mm(left_high, right_high, dims) + (
        mm(left_high, right_low, dims) + mm(left_low, right_high, dims)
    )


def triangle(width):
    tiles = width // LANES
    return [(i, j) for i in range(tiles) for j in range(i + 1)]


def column_of(row):
    return jnp.broadcast_to(row, (LANES, LANES)).T


def offset_of(me, levels):
    return sum(((me >> bit) & (members - 1)) * size for bit, members, size in levels)


def eye(size):
    return lax.broadcasted_iota(jnp.int32, (size, size), 0) == lax.broadcasted_iota(
        jnp.int32, (size, size), 1
    )


def code_floats(value):
    size = jnp.abs(value.astype(F32))
    power = jnp.floor(jnp.log2(jnp.maximum(size, 2.0**-126)))
    mantissa = size * jnp.exp2(-power)
    power = power + jnp.where(mantissa >= 2.0, 1.0, 0.0) - jnp.where(mantissa < 1.0, 1.0, 0.0)
    mantissa = jnp.where(
        mantissa >= 2.0, mantissa * 0.5, jnp.where(mantissa < 1.0, mantissa * 2.0, mantissa)
    )
    code = (power + 127.0) * 128.0 + jnp.round((mantissa - 1.0) * 128.0)
    code = jnp.where(size < 2.0**-126, 0.0, code)
    return jnp.where(value.astype(F32) < 0.0, -code, code)


def float_of(code):
    size = jnp.abs(code)
    power = lax.shift_right_logical(size, 7).astype(F32) - 127.0
    value = (1.0 + (size & 127).astype(F32) / 128.0) * jnp.exp2(power)
    value = jnp.where(size == 0, 0.0, value)
    return jnp.where(code < 0, -value, value)


def decode(codes_ref, scale_ref, start, target_ref):
    rows, width = target_ref.shape
    for g in range(rows // LANES):
        index = scale_ref[pl.ds(start // LANES + g, 1), :]
        scale = column_of(jnp.exp2(index.astype(F32) / 16.0) / 128.0)
        at = pl.multiple_of(start + g * LANES, LANES)
        for c in range(width // LANES):
            cols = slice(c * LANES, (c + 1) * LANES)
            value = codes_ref[pl.ds(at, LANES), cols].astype(F32) * scale
            target_ref[g * LANES : (g + 1) * LANES, cols] = value.astype(BF16)


def gram_kernel(
    weight_store,
    weight_new,
    me_ref,
    lengths_ref,
    scale_ref,
    queries_ref,
    act_hbm,
    grad_hbm,
    basis_in_hbm,
    basis_out_hbm,
    codes_hbm,
    new_rows_ref,
    keep_ref,
    send_ref,
    diag_ref,
    asked_ref,
    act,
    grad,
    basis_in,
    basis_out,
    codes,
    stored,
    stored_next,
    total,
    sems,
    code_sems,
):
    rows, width = codes.shape
    rank = basis_in.shape[0]
    tokens = act.shape[0]
    examples = new_rows_ref.shape[0]
    chunk = stored.shape[0]
    cuts = 4
    span = grad.shape[1] // cuts
    parts = [(basis_out_hbm, basis_out)]
    for c in range(cuts):
        at = (slice(None), slice(c * span, (c + 1) * span))
        parts.append((grad_hbm.at[at], grad.at[at]))
    parts += [(basis_in_hbm, basis_in), (act_hbm, act)]
    copies = [
        pltpu.make_async_copy(source, target, sems.at[i])
        for i, (source, target) in enumerate(parts)
    ]

    def code_copy(c):
        at = pl.ds(pl.multiple_of(c * chunk, chunk), chunk)
        return pltpu.make_async_copy(codes_hbm.at[at, :], codes.at[at, :], code_sems.at[c])

    chunks = rows // chunk
    for c in range(chunks // 2):
        code_copy(c).start()
    for copy in copies:
        copy.start()
    for c in range(chunks // 2, chunks):
        code_copy(c).start()
    asked = code_floats(queries_ref[...])
    asked = [asked[:, i * LANES : (i + 1) * LANES] for i in range(width // LANES)]
    asked_ref[...] = jnp.concatenate(asked, axis=0).astype(jnp.int32).astype(jnp.int16)
    side = 256

    def ready(c, target):
        code_copy(c).wait()
        decode(codes, scale_ref, c * chunk, target)

    def add(source, first):
        for i in range(width // side):
            at = slice(i * side, (i + 1) * side)
            to = slice(0, (i + 1) * side)
            value = mm(source[:, at], source[:, to], TN)
            total[at, to] = value if first else total[at, to] + value

    ready(0, stored)
    ready(1, stored_next)
    add(stored, True)

    def body(pair, _):
        ready(2 * pair + 2, stored)
        add(stored_next, False)
        ready(2 * pair + 3, stored_next)
        add(stored, False)
        return 0

    lax.fori_loop(0, chunks // 4 - 1, body, 0)
    copies[0].wait()
    proj_out = jnp.zeros((tokens, rank), F32)
    for c in range(cuts):
        copies[1 + c].wait()
        at = (slice(None), slice(c * span, (c + 1) * span))
        proj_out = proj_out + mm(grad[at], basis_out[at], NT)
    copies[-2].wait()
    copies[-1].wait()
    proj_in = mm(act[...], basis_in[...], NT)
    wide = (3 * rank, width)
    k = lax.broadcasted_iota(jnp.int32, wide, 0) & (rank - 1)
    c = lax.broadcasted_iota(jnp.int32, wide, 1)
    pick_in = (k == lax.shift_right_logical(c, rank.bit_length() - 1)).astype(F32).astype(BF16)
    pick_out = (k == (c & (rank - 1))).astype(F32).astype(BF16)
    left = mm(jnp.concatenate(split3(proj_in), axis=1), pick_in)
    right = mm(jnp.concatenate(split3(proj_out), axis=1), pick_out)
    products = split3(left * right)
    place = lax.broadcasted_iota(jnp.int32, (examples, tokens), 1)
    owner = lax.broadcasted_iota(jnp.int32, (examples, tokens), 0)
    member = jnp.zeros((examples, tokens), F32)
    start = jnp.int32(0)
    for e in range(examples):
        finish = start + lengths_ref[0, e]
        inside = (owner == e) & (place >= start) & (place < finish)
        member = jnp.where(inside, 1.0, member)
        start = finish
    member = member.astype(BF16)
    new_rows = mm(member, products[0]) + (mm(member, products[1]) + mm(member, products[2]))
    new_rows_ref[...] = new_rows
    high, mid, low = [part.astype(F32) for part in split3(new_rows)]
    first = jnp.concatenate([high, high, mid, high, low, mid], axis=0).astype(BF16)
    second = jnp.concatenate([high, mid, high, low, high, mid], axis=0).astype(BF16)
    lax.fori_loop(chunks // 4 - 1, chunks // 2 - 1, body, 0)
    add(stored_next, False)
    tiles = triangle(width)
    half = len(tiles) // 2
    diagonal = eye(LANES)

    def finish(mine):
        for i in range(width // side):
            for j in range(i + 1):
                down = slice(i * side, (i + 1) * side)
                across = slice(j * side, (j + 1) * side)
                value = weight_store * total[down, across] + weight_new * mm(
                    first[:, down], second[:, across], TN
                )
                for b, (p, q) in enumerate(tiles):
                    if p // 2 != i or q // 2 != j:
                        continue
                    tile = value[
                        p % 2 * LANES : (p % 2 + 1) * LANES, q % 2 * LANES : (q % 2 + 1) * LANES
                    ]
                    target = keep_ref if b // half == mine else send_ref
                    target[b % half * LANES : (b % half + 1) * LANES, :] = tile
                    if p == q:
                        diag_ref[p : p + 1, :] = jnp.sum(
                            jnp.where(diagonal, tile, 0.0), axis=0, keepdims=True
                        )

    for mine in range(2):
        pl.when((me_ref[0] & 1) == mine)(functools.partial(finish, mine))
    send_ref[half * LANES :, :] = diag_ref[...]


def gram(
    me, lengths, codes, scale_index, queries, activations, out_grads, basis_in, basis_out, count
):
    rows, width = codes.shape
    examples = lengths.shape[1]
    half = len(triangle(width)) // 2 * LANES
    chunk = 256
    extra = width // LANES
    return pl.pallas_call(
        functools.partial(gram_kernel, 0.75 / (count * rows), 0.25 / (count * examples)),
        in_specs=[SMEM, SMEM, VMEM, VMEM] + [ANY] * 5,
        out_specs=[VMEM] * 5,
        out_shape=[
            jax.ShapeDtypeStruct((examples, width), F32),
            jax.ShapeDtypeStruct((half, LANES), F32),
            jax.ShapeDtypeStruct((half + extra, LANES), F32),
            jax.ShapeDtypeStruct((extra, LANES), F32),
            jax.ShapeDtypeStruct((queries.shape[0] * extra, LANES), jnp.int16),
        ],
        scratch_shapes=[
            pltpu.VMEM(activations.shape, BF16),
            pltpu.VMEM(out_grads.shape, BF16),
            pltpu.VMEM(basis_in.shape, BF16),
            pltpu.VMEM(basis_out.shape, BF16),
            pltpu.VMEM((rows, width), jnp.int32),
            pltpu.VMEM((chunk, width), BF16),
            pltpu.VMEM((chunk, width), BF16),
            pltpu.VMEM((width, width), F32),
            pltpu.SemaphoreType.DMA((8,)),
            pltpu.SemaphoreType.DMA((rows // chunk,)),
        ],
        compiler_params=pltpu.CompilerParams(vmem_limit_bytes=57 << 20),
        cost_estimate=pl.CostEstimate(
            flops=6 * 10**9, bytes_accessed=30 * 10**6, transcendentals=0
        ),
        name="fisher_share",
    )(
        me,
        lengths,
        scale_index,
        queries,
        activations,
        out_grads,
        basis_in,
        basis_out,
        codes,
    )


def exponents(diag):
    return jnp.clip(jnp.ceil(32.0 * jnp.log2(jnp.maximum(diag, 1e-30))), -4000.0, 4000.0)


def fill_scales(exps, factor, columns, rows_ref):
    scale = jnp.exp2(exps / 64.0)
    rows_ref[...] = scale * factor
    for t in range(exps.shape[0]):
        columns[t * LANES : (t + 1) * LANES, :] = column_of(scale[t : t + 1, :])


def read_exps(ref, start, tiles):
    return ref[start : start + PACK, :].astype(jnp.int32).astype(F32)[:tiles, :]


def write_exps(ref, start, exps):
    tiles = exps.shape[0]
    padded = jnp.concatenate([exps, jnp.zeros((PACK - tiles, LANES), F32)], axis=0)
    ref[start : start + PACK, :] = padded.astype(jnp.int32).astype(jnp.int16)


def encode(value, inverse):
    scaled = jnp.clip(jnp.round(value * inverse), -CODE_MAX, CODE_MAX)
    return scaled.astype(jnp.int32).astype(jnp.int16)


def strip_scale(table_ref, columns, rows_ref, flat, strip):
    tile = flat // LANES
    i = table_ref[0, tile]
    j = table_ref[1, tile]
    at = pl.multiple_of(i * LANES + flat % LANES, strip)
    return columns[pl.ds(at, strip), :] * rows_ref[pl.ds(j, 1), :]


def combine_kernel(levels, bit, members, has_own, coded, tiles, strip, *refs):
    me_ref, table_ref = refs[:2]
    refs = refs[2:]
    if has_own:
        (own_ref, state_ref), refs = refs[:2], refs[2:]
    arrived, refs = refs[:coded], refs[coded:]
    if members < 2:
        asked_ref, refs = refs[0], refs[1:]
    if members > 1:
        (out_own, out_state), refs = refs[:2], refs[2:]
        targets, refs = refs[: members - 1], refs[members - 1 :]
    else:
        (out_own, out_state), refs = refs[:2], refs[2:]
        targets = [out_own]
    columns, rows_ref, inverse_columns, inverse_rows = refs
    extra = asked_ref.shape[0] if members < 2 else 0
    rows = (out_own.shape[0] - (PACK if members else 0) - extra) if members < 2 else (
        own_ref.shape[0]
    )
    if not members and not has_own:
        rows = out_own.shape[0] - 2 * extra
    if arrived[0].dtype == F32:
        exps = exponents(state_ref[...] + arrived[0][rows:, :])
    else:
        theirs = [read_exps(ref, rows, tiles) for ref in arrived]
        known = [read_exps(state_ref, 0, tiles)] if has_own else []
        level = [jnp.exp2(e / 32.0) for e in known + theirs]
        while len(level) > 1:
            level = [a + b for a, b in zip(level[::2], level[1::2])]
        exps = exponents(level[0])
        for m, e in enumerate(theirs):
            fill_scales(e, 1.0 / CODE_MAX, columns.at[m], rows_ref.at[m])
    fill_scales(-exps, CODE_MAX, inverse_columns, inverse_rows)
    base = offset_of(me_ref[0], levels)
    mine_at = (me_ref[0] >> bit) & (members - 1) if members > 1 else 0
    part = rows // max(members, 1)
    for m in range(max(members, 1)):
        first = (mine_at ^ m) * part

        def body(s, _):
            inside = pl.multiple_of(s * strip, strip)
            at = pl.multiple_of(first + inside, strip)
            flat = base + at
            value = own_ref[pl.ds(at, strip), :] if has_own else 0.0
            for a, ref in enumerate(arrived):
                got = ref[pl.ds(at, strip), :]
                if got.dtype == F32:
                    value = value + got
                else:
                    got = got.astype(jnp.int32).astype(F32)
                    value = value + got * strip_scale(
                        table_ref, columns.at[a], rows_ref.at[a], flat, strip
                    )
            if members > 1 and m == 0:
                out_own[pl.ds(inside, strip), :] = value
            else:
                inverse = strip_scale(table_ref, inverse_columns, inverse_rows, flat, strip)
                target = targets[max(m - 1, 0)]
                target[pl.ds(inside, strip), :] = encode(value, inverse)
            return 0

        lax.fori_loop(0, part // strip, body, 0, unroll=2)
    write_exps(out_state, 0, exps)
    if members:
        for ref in targets:
            write_exps(ref, part, exps)
    if members == 1:
        out_own[rows + PACK :, :] = asked_ref[...]
    elif not members and has_own:
        out_own[rows:, :] = asked_ref[...]
    elif not members:
        out_own[rows : rows + extra, :] = asked_ref[...]
        out_own[rows + extra :, :] = arrived[1][rows + PACK :, :]


def combine(me, table, levels, rows, own, arrived, bit, members, strip, asked):
    tiles = table.shape[1]
    width_tiles = int(round(((8 * tiles + 1) ** 0.5 - 1) / 2))
    width = width_tiles * LANES
    part = rows // max(members, 1)
    short = jnp.int16
    state = jax.ShapeDtypeStruct((PACK, LANES), short)
    if members > 1:
        message = jax.ShapeDtypeStruct((part + PACK, LANES), short)
        outs = [jax.ShapeDtypeStruct((part, LANES), F32), state] + [message] * (members - 1)
        more = []
    else:
        extra = asked.shape[0]
        size = rows + (PACK + extra if members else extra if own else 2 * extra)
        outs = [jax.ShapeDtypeStruct((size, LANES), short), state]
        more = [asked]
    operands = [*own, *arrived, *more]
    return pl.pallas_call(
        functools.partial(
            combine_kernel,
            levels,
            bit,
            members,
            bool(own),
            len(arrived),
            width_tiles,
            strip,
        ),
        in_specs=[SMEM, SMEM] + [VMEM] * len(operands),
        out_specs=[VMEM] * len(outs),
        out_shape=outs,
        scratch_shapes=[
            pltpu.VMEM((len(arrived), width, LANES), F32),
            pltpu.VMEM((len(arrived), width_tiles, LANES), F32),
            pltpu.VMEM((width, LANES), F32),
            pltpu.VMEM((width_tiles, LANES), F32),
        ],
        compiler_params=pltpu.CompilerParams(vmem_limit_bytes=32 << 20),
        cost_estimate=pl.CostEstimate(
            flops=10 * rows * LANES, bytes_accessed=8 * rows * LANES, transcendentals=0
        ),
        name="sum_shares",
    )(me, table, *operands)


def solve_kernel(
    side,
    levels,
    masks,
    count,
    slot_bits,
    me_ref,
    first_ref,
    second_ref,
    state_ref,
    new_rows_ref,
    scale_ref,
    codes_hbm,
    scores_hbm,
    new_scores_ref,
    flat,
    system,
    pair,
    stored,
    solved,
    columns,
    rows_ref,
    codes,
    scores,
    sems,
    out_sems,
):
    lots = sems.shape[0]
    lot = codes.shape[0] // lots

    def fetch(c):
        at = pl.ds(pl.multiple_of(c * lot, lot), lot)
        return pltpu.make_async_copy(codes_hbm.at[at, :], codes.at[at, :], sems.at[c])

    for c in range(lots):
        fetch(c).start()
    queries, width = solved.shape
    tiles = width // LANES
    pieces = len(masks)
    piece = flat.shape[0] // pieces
    pitch = 2 * first_ref.shape[0] // pieces
    asked = []
    for p in range(pieces):
        source = first_ref if p < pieces // 2 else second_ref
        at = p % (pieces // 2) * pitch
        place = pl.multiple_of(offset_of(me_ref[0] ^ masks[p], levels), PACK)
        flat[pl.ds(place, piece), :] = source[at : at + piece, :]
        asked.append(source[at + piece : at + pitch, :].astype(jnp.int32))
    asked = float_of(jnp.concatenate(asked, axis=0)).astype(BF16)
    each = queries // count
    packet = each * tiles
    order = (tiles * queries, asked.shape[0])
    to = lax.broadcasted_iota(jnp.int32, order, 0)
    source = lax.broadcasted_iota(jnp.int32, order, 1)
    slot = lax.shift_right_logical(source, packet.bit_length() - 1)
    owner = jnp.zeros(order, jnp.int32)
    for bit, position in enumerate(slot_bits):
        owner = owner | ((lax.shift_right_logical(slot, position) & 1) << bit)
    owner = owner ^ me_ref[0]
    inside = source & (packet - 1)
    target = (
        lax.shift_right_logical(inside, each.bit_length() - 1) * queries
        + owner * each
        + (inside & (each - 1))
    )
    asked = mm((target == to).astype(F32).astype(BF16), asked)
    for i in range(tiles):
        system[width:, i * LANES : (i + 1) * LANES] = asked[i * queries : (i + 1) * queries, :]
    fill_scales(read_exps(state_ref, 0, tiles), 1.0 / CODE_MAX, columns, rows_ref)
    diagonal = eye(LANES)
    trace = jnp.zeros((1, LANES), F32)
    for b, (i, j) in enumerate(triangle(width)):
        value = flat[b * LANES : (b + 1) * LANES, :].astype(jnp.int32).astype(F32)
        value = value * columns[i * LANES : (i + 1) * LANES, :] * rows_ref[j : j + 1, :]
        system[i * LANES : (i + 1) * LANES, j * LANES : (j + 1) * LANES] = value
        if i == j:
            trace = trace + jnp.sum(jnp.where(diagonal, value, 0.0), axis=0, keepdims=True)
        elif i * LANES // side == j * LANES // side:
            system[j * LANES : (j + 1) * LANES, i * LANES : (i + 1) * LANES] = value.T
    damp = (0.1 / width) * jnp.sum(trace)
    for i in range(tiles):
        at = slice(i * LANES, (i + 1) * LANES)
        system[at, at] += jnp.where(diagonal, damp, 0.0)
    blocks = width // side
    spans = [slice(b * side, (b + 1) * side) for b in range(blocks)]
    unit = eye(side)
    def await_lot(c):
        @pl.when(c < lots)
        def _():
            fetch(c).wait()

    def decode_lot(c):
        start = pl.multiple_of(jnp.minimum(c, lots - 1) * lot, lot)
        decode(codes, scale_ref, start, stored.at[pl.ds(start, lot), :])

    taken = jnp.int32(0)
    for b, span in enumerate(spans):
        below = (b + 1) * side
        block = system[span, span]
        bound = jnp.max(jnp.sum(jnp.abs(block), axis=0, keepdims=True))
        low = damp / bound

        def step_from(value, low):
            gain = 4.0 / ((1.0 + low) * (1.0 + low))
            return gain, jnp.where(unit, gain * (1.0 + low), 0.0) - gain * value

        block = block * (1.0 / bound)
        gain, step = step_from(block, low)
        pair[:side, :] = step * (1.0 / bound)
        pair[side:, :] = mm3(split2(block), split2(step))

        def more(carry):
            return carry[0] < 0.95

        def newton(carry):
            low, taken = carry
            await_lot(taken)
            both = pair[...]
            gain, step = step_from(both[side:, :], low)
            decode_lot(taken)
            pair[...] = mm3(split2(both), split2(step))
            return gain * low, taken + 1

        low, taken = lax.while_loop(more, newton, (gain * low, taken))
        both = pair[...]
        gain, step = step_from(both[side:, :], low)
        low = gain * low
        inverse = split2(mm3(split2(both[:side, :]), split2(step)) * (2.0 / (1.0 + low)))
        panel = system[below:, span]
        weights = split2(mm3(split2(panel), inverse))
        later = split2(panel[: width - below, :])
        system[below:, span] = weights[0].astype(F32) + weights[1].astype(F32)
        for c in range(b + 1, blocks):
            from_row = c * side - below
            update = mm3(
                (weights[0][from_row:, :], weights[1][from_row:, :]),
                (
                    later[0][from_row : from_row + side, :],
                    later[1][from_row : from_row + side, :],
                ),
                NT,
            )
            system[c * side :, spans[c]] -= update
    for b in reversed(range(blocks)):
        below = (b + 1) * side
        value = system[width:, spans[b]]
        if below < width:
            value = value - mm3(
                split2(solved[:, below:]), split2(system[below:width, spans[b]])
            )
        solved[:, spans[b]] = value
    high, low = split2(solved[...])
    new_scores_ref[...] = mm3(split2(new_rows_ref[...]), (high, low), NT)
    both = jnp.concatenate([high, low], axis=0)

    def rest(c, _):
        fetch(c).wait()
        decode_lot(c)
        return 0

    lax.fori_loop(taken, lots, rest, 0)
    span = scores.shape[1] // out_sems.shape[0]
    copies = []
    for c in range(out_sems.shape[0]):
        at = slice(c * span, (c + 1) * span)
        value = mm(both, stored[at, :], NT)
        scores[:, at] = value[:queries, :] + value[queries:, :]
        out = pltpu.make_async_copy(scores.at[:, at], scores_hbm.at[:, at], out_sems.at[c])
        out.start()
        copies.append(out)
    for out in copies:
        out.wait()


def solve(
    me, levels, masks, count, slot_bits, first, second, state, new_rows, scale_index, codes, asked
):
    rows, width = codes.shape
    examples = new_rows.shape[0]
    side = 256
    flat_rows = len(triangle(width)) * LANES
    return pl.pallas_call(
        functools.partial(solve_kernel, side, levels, masks, count, slot_bits),
        in_specs=[SMEM] + [VMEM] * 5 + [ANY],
        out_specs=[ANY, VMEM],
        out_shape=[
            jax.ShapeDtypeStruct((asked, rows), F32),
            jax.ShapeDtypeStruct((examples, asked), F32),
        ],
        scratch_shapes=[
            pltpu.VMEM((flat_rows, LANES), jnp.int16),
            pltpu.VMEM((width + asked, width), F32),
            pltpu.VMEM((2 * side, side), F32),
            pltpu.VMEM((rows, width), BF16),
            pltpu.VMEM((asked, width), F32),
            pltpu.VMEM((width, LANES), F32),
            pltpu.VMEM((width // LANES, LANES), F32),
            pltpu.VMEM((rows, width), jnp.int32),
            pltpu.VMEM((asked, rows), F32),
            pltpu.SemaphoreType.DMA((rows // (2 * LANES),)),
            pltpu.SemaphoreType.DMA((8,)),
        ],
        compiler_params=pltpu.CompilerParams(vmem_limit_bytes=46 << 20),
        cost_estimate=pl.CostEstimate(
            flops=10 * 10**9, bytes_accessed=20 * 10**6, transcendentals=0
        ),
        name="solve_and_score",
    )(me, first, second, state, new_rows, scale_index, codes)


def swap(value, mask, count):
    return lax.ppermute(value, "store", [(i, i ^ mask) for i in range(count)])


def shards(activations, out_grads, basis_in, basis_out, lengths, codes, scale_index, queries):
    count = lax.axis_size("store")
    me = lax.axis_index("store").astype(jnp.int32)[None]
    width = codes.shape[1]
    tiles = triangle(width)
    table = np.array(tiles, np.int32).T
    scale_index = scale_index.reshape(-1, LANES)
    new_rows, own, send, state, asked = gram(
        me,
        lengths,
        codes,
        scale_index,
        queries,
        activations,
        out_grads,
        basis_in,
        basis_out,
        count,
    )
    groups = []
    bit = 1
    while 1 << bit < count:
        members = 4 if 1 << (bit + 1) < count else 2
        groups.append((bit, members))
        bit += 2
    piece = len(tiles) * LANES // count
    strip = int(np.gcd(np.gcd(piece, LANES), 64))
    arrived = [swap(send, 1, count)]
    rows = own.shape[0]
    levels = [(0, 2, rows)]
    own = [own, state]
    for bit, members in groups:
        if members == 2:
            coded, _ = combine(me, table, levels, rows, own, arrived, bit, 1, strip, asked)
            own, arrived = [], [coded, swap(coded, 1 << bit, count)]
            break
        own = combine(me, table, levels, rows, own, arrived, bit, members, strip, asked)
        own, messages = own[:2], own[2:]
        arrived = [swap(message, (m + 1) << bit, count) for m, message in enumerate(messages)]
        rows //= members
        levels = levels + [(bit, members, rows)]
    final, state = combine(me, table, levels, rows, own, arrived, 0, 0, strip, asked)
    for bit, members in reversed(groups):
        if members > 2:
            final = jnp.concatenate(
                [final] + [swap(final, m << bit, count) for m in range(1, members)], axis=0
            )
    other = swap(final, 1, count)
    slot_bits = [count.bit_length() - 2]
    for bit, members in groups:
        for low in range(members // 2):
            slot_bits.append(slot_bits[0] - (bit + members // 2 - 1) + low)
    packets = len(tiles) * LANES // rows
    masks = []
    for slot in range(packets):
        first = slot * (count // packets)
        masks.append(sum((first >> position & 1) << b for b, position in enumerate(slot_bits)))
    scores, new_scores = solve(
        me,
        levels,
        masks,
        count,
        slot_bits,
        final,
        other,
        state,
        new_rows,
        scale_index,
        codes,
        count * queries.shape[0],
    )
    return new_rows, scores, new_scores.T


def solution(mesh):
    return jax.shard_map(
        shards,
        mesh=mesh,
        in_specs=(
            P(("groups", "store"), None),
            P(("groups", "store"), None),
            P(),
            P(),
            P(("groups", "store"), None),
            P(("groups", "store"), None),
            P(("groups", "store")),
            P(("groups", "store"), None),
        ),
        out_specs=(P(("groups", "store"), None), P("groups", "store"), P("groups", "store")),
        check_vma=False,
    )
```

```python
import functools

import jax
import jax.numpy as jnp
import numpy as np
from jax import lax
from jax.experimental import pallas as pl
from jax.experimental.pallas import tpu as pltpu
from jax.sharding import PartitionSpec as P

LANES = 128
PACK = 16
CODE_MAX = 32767.0
F32 = jnp.float32
BF16 = jnp.bfloat16
VMEM = pl.BlockSpec(memory_space=pltpu.VMEM)
SMEM = pl.BlockSpec(memory_space=pltpu.SMEM)
ANY = pl.BlockSpec(memory_space=pl.ANY)
NN = (((1,), (0,)), ((), ()))
NT = (((1,), (1,)), ((), ()))
TN = (((0,), (0,)), ((), ()))


def mm(left, right, dims=NN):
    return lax.dot_general(left, right, dims, preferred_element_type=F32)


def split2(value):
    high = value.astype(BF16)
    return high, (value - high.astype(F32)).astype(BF16)


def split3(value):
    high, _ = split2(value)
    rest = value - high.astype(F32)
    mid, low = split2(rest)
    return high, mid, low


def mm3(left, right, dims=NN):
    left_high, left_low = left
    right_high, right_low = right
    return mm(left_high, right_high, dims) + (
        mm(left_high, right_low, dims) + mm(left_low, right_high, dims)
    )


def mm6(left, right, dims=NN):
    left_high, left_mid, left_low = left
    right_high, right_mid, right_low = right
    small = mm(left_high, right_low, dims) + mm(left_low, right_high, dims)
    small = small + mm(left_mid, right_mid, dims)
    middle = mm(left_high, right_mid, dims) + mm(left_mid, right_high, dims)
    return mm(left_high, right_high, dims) + (middle + small)


def triangle(width):
    tiles = width // LANES
    return [(i, j) for i in range(tiles) for j in range(i + 1)]


def column_of(row):
    return jnp.broadcast_to(row, (LANES, LANES)).T


def offset_of(me, levels):
    return sum(((me >> bit) & (members - 1)) * size for bit, members, size in levels)


def eye(size):
    return lax.broadcasted_iota(jnp.int32, (size, size), 0) == lax.broadcasted_iota(
        jnp.int32, (size, size), 1
    )


def code_floats(value):
    size = jnp.abs(value.astype(F32))
    power = jnp.floor(jnp.log2(jnp.maximum(size, 2.0**-126)))
    mantissa = size * jnp.exp2(-power)
    power = power + jnp.where(mantissa >= 2.0, 1.0, 0.0) - jnp.where(mantissa < 1.0, 1.0, 0.0)
    mantissa = jnp.where(
        mantissa >= 2.0, mantissa * 0.5, jnp.where(mantissa < 1.0, mantissa * 2.0, mantissa)
    )
    code = (power + 127.0) * 128.0 + jnp.round((mantissa - 1.0) * 128.0)
    code = jnp.where(size < 2.0**-126, 0.0, code)
    return jnp.where(value.astype(F32) < 0.0, -code, code)


def float_of(code):
    size = jnp.abs(code)
    power = lax.shift_right_logical(size, 7).astype(F32) - 127.0
    value = (1.0 + (size & 127).astype(F32) / 128.0) * jnp.exp2(power)
    value = jnp.where(size == 0, 0.0, value)
    return jnp.where(code < 0, -value, value)


def decode(codes_ref, scale_ref, start, target_ref):
    rows, width = target_ref.shape
    for g in range(rows // LANES):
        index = scale_ref[pl.ds(start // LANES + g, 1), :]
        scale = column_of(jnp.exp2(index.astype(F32) / 16.0) / 128.0)
        at = pl.multiple_of(start + g * LANES, LANES)
        for c in range(width // LANES):
            cols = slice(c * LANES, (c + 1) * LANES)
            value = codes_ref[pl.ds(at, LANES), cols].astype(F32) * scale
            target_ref[g * LANES : (g + 1) * LANES, cols] = value.astype(BF16)


def gram_kernel(
    weight_store,
    weight_new,
    me_ref,
    lengths_ref,
    scale_ref,
    queries_ref,
    act_hbm,
    grad_hbm,
    basis_in_hbm,
    basis_out_hbm,
    codes_hbm,
    new_rows_ref,
    keep_ref,
    send_ref,
    diag_ref,
    asked_ref,
    act,
    grad,
    basis_in,
    basis_out,
    codes,
    stored,
    stored_next,
    total,
    sems,
    code_sems,
):
    rows, width = codes.shape
    rank = basis_in.shape[0]
    tokens = act.shape[0]
    examples = new_rows_ref.shape[0]
    chunk = stored.shape[0]
    cuts = 4
    span = grad.shape[1] // cuts
    parts = [(basis_out_hbm, basis_out)]
    for c in range(cuts):
        at = (slice(None), slice(c * span, (c + 1) * span))
        parts.append((grad_hbm.at[at], grad.at[at]))
    parts += [(basis_in_hbm, basis_in), (act_hbm, act)]
    copies = [
        pltpu.make_async_copy(source, target, sems.at[i])
        for i, (source, target) in enumerate(parts)
    ]

    def code_copy(c):
        at = pl.ds(pl.multiple_of(c * chunk, chunk), chunk)
        return pltpu.make_async_copy(codes_hbm.at[at, :], codes.at[at, :], code_sems.at[c])

    chunks = rows // chunk
    for c in range(chunks // 2):
        code_copy(c).start()
    for copy in copies:
        copy.start()
    for c in range(chunks // 2, chunks):
        code_copy(c).start()
    asked = code_floats(queries_ref[...])
    asked = [asked[:, i * LANES : (i + 1) * LANES] for i in range(width // LANES)]
    asked_ref[...] = jnp.concatenate(asked, axis=0).astype(jnp.int32).astype(jnp.int16)
    side = 256

    def ready(c, target):
        code_copy(c).wait()
        decode(codes, scale_ref, c * chunk, target)

    def add(source, first):
        for i in range(width // side):
            at = slice(i * side, (i + 1) * side)
            to = slice(0, (i + 1) * side)
            value = mm(source[:, at], source[:, to], TN)
            total[at, to] = value if first else total[at, to] + value

    ready(0, stored)
    ready(1, stored_next)
    add(stored, True)

    def body(pair, _):
        ready(2 * pair + 2, stored)
        add(stored_next, False)
        ready(2 * pair + 3, stored_next)
        add(stored, False)
        return 0

    lax.fori_loop(0, chunks // 4 - 1, body, 0)
    copies[0].wait()
    proj_out = jnp.zeros((tokens, rank), F32)
    for c in range(cuts):
        copies[1 + c].wait()
        at = (slice(None), slice(c * span, (c + 1) * span))
        proj_out = proj_out + mm(grad[at], basis_out[at], NT)
    copies[-2].wait()
    copies[-1].wait()
    proj_in = mm(act[...], basis_in[...], NT)
    wide = (3 * rank, width)
    k = lax.broadcasted_iota(jnp.int32, wide, 0) & (rank - 1)
    c = lax.broadcasted_iota(jnp.int32, wide, 1)
    pick_in = (k == lax.shift_right_logical(c, rank.bit_length() - 1)).astype(F32).astype(BF16)
    pick_out = (k == (c & (rank - 1))).astype(F32).astype(BF16)
    left = mm(jnp.concatenate(split3(proj_in), axis=1), pick_in)
    right = mm(jnp.concatenate(split3(proj_out), axis=1), pick_out)
    products = split3(left * right)
    place = lax.broadcasted_iota(jnp.int32, (examples, tokens), 1)
    owner = lax.broadcasted_iota(jnp.int32, (examples, tokens), 0)
    member = jnp.zeros((examples, tokens), F32)
    start = jnp.int32(0)
    for e in range(examples):
        finish = start + lengths_ref[0, e]
        inside = (owner == e) & (place >= start) & (place < finish)
        member = jnp.where(inside, 1.0, member)
        start = finish
    member = member.astype(BF16)
    new_rows = mm(member, products[0]) + (mm(member, products[1]) + mm(member, products[2]))
    new_rows_ref[...] = new_rows
    high, mid, low = [part.astype(F32) for part in split3(new_rows)]
    first = jnp.concatenate([high, high, mid, high, low, mid], axis=0).astype(BF16)
    second = jnp.concatenate([high, mid, high, low, high, mid], axis=0).astype(BF16)
    lax.fori_loop(chunks // 4 - 1, chunks // 2 - 1, body, 0)
    add(stored_next, False)
    tiles = triangle(width)
    half = len(tiles) // 2
    diagonal = eye(LANES)

    def finish(mine):
        for i in range(width // side):
            for j in range(i + 1):
                down = slice(i * side, (i + 1) * side)
                across = slice(j * side, (j + 1) * side)
                value = weight_store * total[down, across] + weight_new * mm(
                    first[:, down], second[:, across], TN
                )
                for b, (p, q) in enumerate(tiles):
                    if p // 2 != i or q // 2 != j:
                        continue
                    tile = value[
                        p % 2 * LANES : (p % 2 + 1) * LANES, q % 2 * LANES : (q % 2 + 1) * LANES
                    ]
                    target = keep_ref if b // half == mine else send_ref
                    target[b % half * LANES : (b % half + 1) * LANES, :] = tile
                    if p == q:
                        diag_ref[p : p + 1, :] = jnp.sum(
                            jnp.where(diagonal, tile, 0.0), axis=0, keepdims=True
                        )

    for mine in range(2):
        pl.when((me_ref[0] & 1) == mine)(functools.partial(finish, mine))
    send_ref[half * LANES :, :] = diag_ref[...]


def gram(
    me, lengths, codes, scale_index, queries, activations, out_grads, basis_in, basis_out, count
):
    rows, width = codes.shape
    examples = lengths.shape[1]
    half = len(triangle(width)) // 2 * LANES
    chunk = 256
    extra = width // LANES
    return pl.pallas_call(
        functools.partial(gram_kernel, 0.75 / (count * rows), 0.25 / (count * examples)),
        in_specs=[SMEM, SMEM, VMEM, VMEM] + [ANY] * 5,
        out_specs=[VMEM] * 5,
        out_shape=[
            jax.ShapeDtypeStruct((examples, width), F32),
            jax.ShapeDtypeStruct((half, LANES), F32),
            jax.ShapeDtypeStruct((half + extra, LANES), F32),
            jax.ShapeDtypeStruct((extra, LANES), F32),
            jax.ShapeDtypeStruct((queries.shape[0] * extra, LANES), jnp.int16),
        ],
        scratch_shapes=[
            pltpu.VMEM(activations.shape, BF16),
            pltpu.VMEM(out_grads.shape, BF16),
            pltpu.VMEM(basis_in.shape, BF16),
            pltpu.VMEM(basis_out.shape, BF16),
            pltpu.VMEM((rows, width), jnp.int32),
            pltpu.VMEM((chunk, width), BF16),
            pltpu.VMEM((chunk, width), BF16),
            pltpu.VMEM((width, width), F32),
            pltpu.SemaphoreType.DMA((8,)),
            pltpu.SemaphoreType.DMA((rows // chunk,)),
        ],
        compiler_params=pltpu.CompilerParams(vmem_limit_bytes=57 << 20),
        cost_estimate=pl.CostEstimate(
            flops=6 * 10**9, bytes_accessed=30 * 10**6, transcendentals=0
        ),
        name="fisher_share",
    )(
        me,
        lengths,
        scale_index,
        queries,
        activations,
        out_grads,
        basis_in,
        basis_out,
        codes,
    )


def exponents(diag):
    return jnp.clip(jnp.ceil(32.0 * jnp.log2(jnp.maximum(diag, 1e-30))), -4000.0, 4000.0)


def fill_scales(exps, factor, columns, rows_ref):
    scale = jnp.exp2(exps / 64.0)
    rows_ref[...] = scale * factor
    for t in range(exps.shape[0]):
        columns[t * LANES : (t + 1) * LANES, :] = column_of(scale[t : t + 1, :])


def read_exps(ref, start, tiles):
    return ref[start : start + PACK, :].astype(jnp.int32).astype(F32)[:tiles, :]


def write_exps(ref, start, exps):
    tiles = exps.shape[0]
    padded = jnp.concatenate([exps, jnp.zeros((PACK - tiles, LANES), F32)], axis=0)
    ref[start : start + PACK, :] = padded.astype(jnp.int32).astype(jnp.int16)


def encode(value, inverse):
    scaled = jnp.clip(jnp.round(value * inverse), -CODE_MAX, CODE_MAX)
    return scaled.astype(jnp.int32).astype(jnp.int16)


def strip_scale(table_ref, columns, rows_ref, flat, strip):
    tile = flat // LANES
    i = table_ref[0, tile]
    j = table_ref[1, tile]
    at = pl.multiple_of(i * LANES + flat % LANES, strip)
    return columns[pl.ds(at, strip), :] * rows_ref[pl.ds(j, 1), :]


def fetch_kernel(first_hbm, second_hbm, first_ref, second_ref, sems):
    copies = [pltpu.make_async_copy(second_hbm, second_ref, sems.at[0])]
    rows = first_ref.shape[0] // 4
    for c in range(4):
        at = pl.ds(c * rows, rows)
        copies.append(
            pltpu.make_async_copy(first_hbm.at[at, :], first_ref.at[at, :], sems.at[c + 1])
        )
    for copy in copies:
        copy.start()
    for copy in copies:
        copy.wait()


def fetch_rows(first, second):
    return pl.pallas_call(
        fetch_kernel,
        in_specs=[ANY, ANY],
        out_specs=[VMEM, VMEM],
        out_shape=[
            jax.ShapeDtypeStruct(first.shape, first.dtype),
            jax.ShapeDtypeStruct(second.shape, second.dtype),
        ],
        scratch_shapes=[pltpu.SemaphoreType.DMA((5,))],
        compiler_params=pltpu.CompilerParams(vmem_limit_bytes=32 << 20),
        cost_estimate=pl.CostEstimate(
            flops=0, bytes_accessed=2 * first.size * first.dtype.itemsize, transcendentals=0
        ),
        name="fetch_rows",
    )(first, second)


def combine_kernel(levels, bit, members, has_own, coded, tiles, strip, *refs):
    me_ref, table_ref = refs[:2]
    refs = refs[2:]
    if has_own:
        (own_ref, state_ref), refs = refs[:2], refs[2:]
    arrived, refs = refs[:coded], refs[coded:]
    if members < 2:
        asked_ref, refs = refs[0], refs[1:]
    if members > 1:
        (out_own, out_state), refs = refs[:2], refs[2:]
        targets, refs = refs[: members - 1], refs[members - 1 :]
    else:
        (out_own, out_state), refs = refs[:2], refs[2:]
        targets = [out_own]
    columns, rows_ref, inverse_columns, inverse_rows = refs
    extra = asked_ref.shape[0] if members < 2 else 0
    rows = (out_own.shape[0] - (PACK if members else 0) - extra) if members < 2 else (
        own_ref.shape[0]
    )
    if not members and not has_own:
        rows = out_own.shape[0] - 2 * extra
    if arrived[0].dtype == F32:
        exps = exponents(state_ref[...] + arrived[0][rows:, :])
    else:
        theirs = [read_exps(ref, rows, tiles) for ref in arrived]
        known = [read_exps(state_ref, 0, tiles)] if has_own else []
        level = [jnp.exp2(e / 32.0) for e in known + theirs]
        while len(level) > 1:
            level = [a + b for a, b in zip(level[::2], level[1::2])]
        exps = exponents(level[0])
        for m, e in enumerate(theirs):
            fill_scales(e, 1.0 / CODE_MAX, columns.at[m], rows_ref.at[m])
    fill_scales(-exps, CODE_MAX, inverse_columns, inverse_rows)
    base = offset_of(me_ref[0], levels)
    mine_at = (me_ref[0] >> bit) & (members - 1) if members > 1 else 0
    part = rows // max(members, 1)
    for m in range(max(members, 1)):
        first = (mine_at ^ m) * part

        def body(s, _):
            inside = pl.multiple_of(s * strip, strip)
            at = pl.multiple_of(first + inside, strip)
            flat = base + at
            value = own_ref[pl.ds(at, strip), :] if has_own else 0.0
            for a, ref in enumerate(arrived):
                got = ref[pl.ds(at, strip), :]
                if got.dtype == F32:
                    value = value + got
                else:
                    got = got.astype(jnp.int32).astype(F32)
                    value = value + got * strip_scale(
                        table_ref, columns.at[a], rows_ref.at[a], flat, strip
                    )
            if members > 1 and m == 0:
                out_own[pl.ds(inside, strip), :] = value
            else:
                inverse = strip_scale(table_ref, inverse_columns, inverse_rows, flat, strip)
                target = targets[max(m - 1, 0)]
                target[pl.ds(inside, strip), :] = encode(value, inverse)
            return 0

        lax.fori_loop(0, part // strip, body, 0, unroll=2)
    write_exps(out_state, 0, exps)
    if members:
        for ref in targets:
            write_exps(ref, part, exps)
    if members == 1:
        out_own[rows + PACK :, :] = asked_ref[...]
    elif not members and has_own:
        out_own[rows:, :] = asked_ref[...]
    elif not members:
        out_own[rows : rows + extra, :] = asked_ref[...]
        out_own[rows + extra :, :] = arrived[1][rows + PACK :, :]


def combine(me, table, levels, rows, own, arrived, bit, members, strip, asked):
    tiles = table.shape[1]
    width_tiles = int(round(((8 * tiles + 1) ** 0.5 - 1) / 2))
    width = width_tiles * LANES
    part = rows // max(members, 1)
    short = jnp.int16
    state = jax.ShapeDtypeStruct((PACK, LANES), short)
    if members > 1:
        message = jax.ShapeDtypeStruct((part + PACK, LANES), short)
        outs = [jax.ShapeDtypeStruct((part, LANES), F32), state] + [message] * (members - 1)
        more = []
    else:
        extra = asked.shape[0]
        size = rows + (PACK + extra if members else extra if own else 2 * extra)
        outs = [jax.ShapeDtypeStruct((size, LANES), short), state]
        more = [asked]
    operands = [*own, *arrived, *more]
    return pl.pallas_call(
        functools.partial(
            combine_kernel,
            levels,
            bit,
            members,
            bool(own),
            len(arrived),
            width_tiles,
            strip,
        ),
        in_specs=[SMEM, SMEM] + [VMEM] * len(operands),
        out_specs=[VMEM] * len(outs),
        out_shape=outs,
        scratch_shapes=[
            pltpu.VMEM((len(arrived), width, LANES), F32),
            pltpu.VMEM((len(arrived), width_tiles, LANES), F32),
            pltpu.VMEM((width, LANES), F32),
            pltpu.VMEM((width_tiles, LANES), F32),
        ],
        compiler_params=pltpu.CompilerParams(vmem_limit_bytes=32 << 20),
        cost_estimate=pl.CostEstimate(
            flops=10 * rows * LANES, bytes_accessed=8 * rows * LANES, transcendentals=0
        ),
        name="sum_shares",
    )(me, table, *operands)


def solve_kernel(
    side,
    levels,
    masks,
    count,
    slot_bits,
    me_ref,
    first_ref,
    second_ref,
    state_ref,
    new_rows_ref,
    scale_ref,
    codes_hbm,
    scores_hbm,
    new_scores_ref,
    flat,
    system,
    pair,
    stored,
    solved,
    columns,
    rows_ref,
    codes,
    scores,
    taken_ref,
    sems,
    out_sems,
):
    lots = sems.shape[0]
    lot = codes.shape[0] // lots

    def fetch(c):
        at = pl.ds(pl.multiple_of(c * lot, lot), lot)
        return pltpu.make_async_copy(codes_hbm.at[at, :], codes.at[at, :], sems.at[c])

    for c in range(lots):
        fetch(c).start()
    queries, width = solved.shape
    tiles = width // LANES
    pieces = len(masks)
    piece = flat.shape[0] // pieces
    pitch = 2 * first_ref.shape[0] // pieces
    asked = []
    for p in range(pieces):
        source = first_ref if p < pieces // 2 else second_ref
        at = p % (pieces // 2) * pitch
        place = pl.multiple_of(offset_of(me_ref[0] ^ masks[p], levels), PACK)
        flat[pl.ds(place, piece), :] = source[at : at + piece, :]
        asked.append(source[at + piece : at + pitch, :].astype(jnp.int32))
    asked = float_of(jnp.concatenate(asked, axis=0)).astype(BF16)
    each = queries // count
    packet = each * tiles
    order = (tiles * queries, asked.shape[0])
    to = lax.broadcasted_iota(jnp.int32, order, 0)
    source = lax.broadcasted_iota(jnp.int32, order, 1)
    slot = lax.shift_right_logical(source, packet.bit_length() - 1)
    owner = jnp.zeros(order, jnp.int32)
    for bit, position in enumerate(slot_bits):
        owner = owner | ((lax.shift_right_logical(slot, position) & 1) << bit)
    owner = owner ^ me_ref[0]
    inside = source & (packet - 1)
    target = (
        lax.shift_right_logical(inside, each.bit_length() - 1) * queries
        + owner * each
        + (inside & (each - 1))
    )
    asked = mm((target == to).astype(F32).astype(BF16), asked)
    for i in range(tiles):
        system[width:, i * LANES : (i + 1) * LANES] = asked[i * queries : (i + 1) * queries, :]
    fill_scales(read_exps(state_ref, 0, tiles), 1.0 / CODE_MAX, columns, rows_ref)
    diagonal = eye(LANES)
    trace = jnp.zeros((1, LANES), F32)
    for b, (i, j) in enumerate(triangle(width)):
        value = flat[b * LANES : (b + 1) * LANES, :].astype(jnp.int32).astype(F32)
        value = value * columns[i * LANES : (i + 1) * LANES, :] * rows_ref[j : j + 1, :]
        system[i * LANES : (i + 1) * LANES, j * LANES : (j + 1) * LANES] = value
        if i == j:
            trace = trace + jnp.sum(jnp.where(diagonal, value, 0.0), axis=0, keepdims=True)
        elif i * LANES // side == j * LANES // side:
            system[j * LANES : (j + 1) * LANES, i * LANES : (i + 1) * LANES] = value.T
    damp = (0.1 / width) * jnp.sum(trace)
    for i in range(tiles):
        at = slice(i * LANES, (i + 1) * LANES)
        system[at, at] += jnp.where(diagonal, damp, 0.0)
    blocks = width // side
    spans = [slice(b * side, (b + 1) * side) for b in range(blocks)]
    unit = eye(side)
    def await_lot(c):
        @pl.when(c < lots)
        def _():
            fetch(c).wait()

    def decode_lot(c):
        start = pl.multiple_of(jnp.minimum(c, lots - 1) * lot, lot)
        decode(codes, scale_ref, start, stored.at[pl.ds(start, lot), :])

    def eliminate(split, mul, refine):
        for b, span in enumerate(spans):
            below = (b + 1) * side
            block = system[span, span]
            bound = jnp.max(jnp.sum(jnp.abs(block), axis=0, keepdims=True))
            low = damp / bound

            def step_from(value, low):
                gain = 4.0 / ((1.0 + low) * (1.0 + low))
                return gain, jnp.where(unit, gain * (1.0 + low), 0.0) - gain * value

            block = block * (1.0 / bound)
            gain, step = step_from(block, low)
            pair[:side, :] = step * (1.0 / bound)
            pair[side:, :] = mul(split(block), split(step))

            def more(low):
                return low < 0.95

            def newton(low):
                taken = taken_ref[0]
                taken_ref[0] = taken + 1
                await_lot(taken)
                both = pair[...]
                gain, step = step_from(both[side:, :], low)
                decode_lot(taken)
                pair[...] = mul(split(both), split(step))
                return gain * low

            low = lax.while_loop(more, newton, gain * low)
            both = pair[...]
            gain, step = step_from(both[side:, :], low)
            low = gain * low
            inverse = mul(split(both[:side, :]), split(step)) * (2.0 / (1.0 + low))
            if refine:
                left = jnp.where(unit, 1.0, 0.0) - mul(split(system[span, span]), split(inverse))
                inverse = inverse + mul(split(inverse), split(left))
            inverse = split(inverse)
            panel = system[below:, span]
            weights = split(mul(split(panel), inverse))
            later = split(panel[: width - below, :])
            system[below:, span] = sum(part.astype(F32) for part in weights)
            for c in range(b + 1, blocks):
                from_row = c * side - below
                update = mul(
                    tuple(part[from_row:, :] for part in weights),
                    tuple(part[from_row : from_row + side, :] for part in later),
                    NT,
                )
                system[c * side :, spans[c]] -= update
        for b in reversed(range(blocks)):
            below = (b + 1) * side
            value = system[width:, spans[b]]
            if below < width:
                value = value - mul(
                    split(solved[:, below:]), split(system[below:width, spans[b]])
                )
            solved[:, spans[b]] = value

    taken_ref[0] = 0
    ratio = jnp.float32(0.0)
    for span in spans:
        sums = jnp.sum(jnp.abs(system[span, span]), axis=0, keepdims=True)
        ratio = jnp.maximum(ratio, jnp.max(sums) / damp)
    pl.when(ratio <= 800.0)(lambda: eliminate(split2, mm3, False))
    pl.when(jnp.logical_not(ratio <= 800.0))(lambda: eliminate(split3, mm6, True))
    high, low = split2(solved[...])
    new_scores_ref[...] = mm3(split2(new_rows_ref[...]), (high, low), NT)
    both = jnp.concatenate([high, low], axis=0)

    def rest(c, _):
        fetch(c).wait()
        decode_lot(c)
        return 0

    lax.fori_loop(jnp.minimum(taken_ref[0], lots), lots, rest, 0)
    span = scores.shape[1] // out_sems.shape[0]
    copies = []
    for c in range(out_sems.shape[0]):
        at = slice(c * span, (c + 1) * span)
        value = mm(both, stored[at, :], NT)
        scores[:, at] = value[:queries, :] + value[queries:, :]
        out = pltpu.make_async_copy(scores.at[:, at], scores_hbm.at[:, at], out_sems.at[c])
        out.start()
        copies.append(out)
    for out in copies:
        out.wait()


def solve(
    me, levels, masks, count, slot_bits, first, second, state, new_rows, scale_index, codes, asked
):
    rows, width = codes.shape
    examples = new_rows.shape[0]
    side = 256
    flat_rows = len(triangle(width)) * LANES
    return pl.pallas_call(
        functools.partial(solve_kernel, side, levels, masks, count, slot_bits),
        in_specs=[SMEM] + [VMEM] * 5 + [ANY],
        out_specs=[ANY, VMEM],
        out_shape=[
            jax.ShapeDtypeStruct((asked, rows), F32),
            jax.ShapeDtypeStruct((examples, asked), F32),
        ],
        scratch_shapes=[
            pltpu.VMEM((flat_rows, LANES), jnp.int16),
            pltpu.VMEM((width + asked, width), F32),
            pltpu.VMEM((2 * side, side), F32),
            pltpu.VMEM((rows, width), BF16),
            pltpu.VMEM((asked, width), F32),
            pltpu.VMEM((width, LANES), F32),
            pltpu.VMEM((width // LANES, LANES), F32),
            pltpu.VMEM((rows, width), jnp.int32),
            pltpu.VMEM((asked, rows), F32),
            pltpu.SMEM((1,), jnp.int32),
            pltpu.SemaphoreType.DMA((rows // (2 * LANES),)),
            pltpu.SemaphoreType.DMA((8,)),
        ],
        compiler_params=pltpu.CompilerParams(vmem_limit_bytes=46 << 20),
        cost_estimate=pl.CostEstimate(
            flops=10 * 10**9, bytes_accessed=20 * 10**6, transcendentals=0
        ),
        name="solve_and_score",
    )(me, first, second, state, new_rows, scale_index, codes)


def swap(value, mask, count):
    return lax.ppermute(value, "store", [(i, i ^ mask) for i in range(count)])


def shards(activations, out_grads, basis_in, basis_out, lengths, codes, scale_index, queries):
    count = lax.axis_size("store")
    me = lax.axis_index("store").astype(jnp.int32)[None]
    width = codes.shape[1]
    tiles = triangle(width)
    table = np.array(tiles, np.int32).T
    scale_index = scale_index.reshape(-1, LANES)
    new_rows, own, send, state, asked = gram(
        me,
        lengths,
        codes,
        scale_index,
        queries,
        activations,
        out_grads,
        basis_in,
        basis_out,
        count,
    )
    groups = []
    bit = 1
    while 1 << bit < count:
        members = 4 if 1 << (bit + 1) < count else 2
        groups.append((bit, members))
        bit += 2
    piece = len(tiles) * LANES // count
    strip = int(np.gcd(np.gcd(piece, LANES), 64))
    arrived = [swap(send, 1, count)]
    rows = own.shape[0]
    levels = [(0, 2, rows)]
    own = fetch_rows(own, state)
    for bit, members in groups:
        if members == 2:
            coded, _ = combine(me, table, levels, rows, own, arrived, bit, 1, strip, asked)
            own, arrived = [], [coded, swap(coded, 1 << bit, count)]
            break
        own = combine(me, table, levels, rows, own, arrived, bit, members, strip, asked)
        own, messages = own[:2], own[2:]
        arrived = [swap(message, (m + 1) << bit, count) for m, message in enumerate(messages)]
        rows //= members
        levels = levels + [(bit, members, rows)]
    final, state = combine(me, table, levels, rows, own, arrived, 0, 0, strip, asked)
    for bit, members in reversed(groups):
        if members > 2:
            final = jnp.concatenate(
                [final] + [swap(final, m << bit, count) for m in range(1, members)], axis=0
            )
    other = swap(final, 1, count)
    slot_bits = [count.bit_length() - 2]
    for bit, members in groups:
        for low in range(members // 2):
            slot_bits.append(slot_bits[0] - (bit + members // 2 - 1) + low)
    packets = len(tiles) * LANES // rows
    masks = []
    for slot in range(packets):
        first = slot * (count // packets)
        masks.append(sum((first >> position & 1) << b for b, position in enumerate(slot_bits)))
    scores, new_scores = solve(
        me,
        levels,
        masks,
        count,
        slot_bits,
        final,
        other,
        state,
        new_rows,
        scale_index,
        codes,
        count * queries.shape[0],
    )
    return new_rows, scores, new_scores.T


def solution(mesh):
    return jax.shard_map(
        shards,
        mesh=mesh,
        in_specs=(
            P(("groups", "store"), None),
            P(("groups", "store"), None),
            P(),
            P(),
            P(("groups", "store"), None),
            P(("groups", "store"), None),
            P(("groups", "store")),
            P(("groups", "store"), None),
        ),
        out_specs=(P(("groups", "store"), None), P("groups", "store"), P("groups", "store")),
        check_vma=False,
    )
```

```python
import functools

import jax
import jax.numpy as jnp
import numpy as np
from jax import lax
from jax.experimental import pallas as pl
from jax.experimental.pallas import tpu as pltpu
from jax.sharding import PartitionSpec as P

LANES = 128
PACK = 16
CODE_MAX = 32767.0
F32 = jnp.float32
BF16 = jnp.bfloat16
VMEM = pl.BlockSpec(memory_space=pltpu.VMEM)
SMEM = pl.BlockSpec(memory_space=pltpu.SMEM)
ANY = pl.BlockSpec(memory_space=pl.ANY)
NN = (((1,), (0,)), ((), ()))
NT = (((1,), (1,)), ((), ()))
TN = (((0,), (0,)), ((), ()))


def mm(left, right, dims=NN):
    return lax.dot_general(left, right, dims, preferred_element_type=F32)


def split2(value):
    high = value.astype(BF16)
    return high, (value - high.astype(F32)).astype(BF16)


def split3(value):
    high, _ = split2(value)
    rest = value - high.astype(F32)
    mid, low = split2(rest)
    return high, mid, low


def mm3(left, right, dims=NN):
    left_high, left_low = left
    right_high, right_low = right
    return mm(left_high, right_high, dims) + (
        mm(left_high, right_low, dims) + mm(left_low, right_high, dims)
    )


def mm6(left, right, dims=NN):
    left_high, left_mid, left_low = left
    right_high, right_mid, right_low = right
    small = mm(left_high, right_low, dims) + mm(left_low, right_high, dims)
    small = small + mm(left_mid, right_mid, dims)
    middle = mm(left_high, right_mid, dims) + mm(left_mid, right_high, dims)
    return mm(left_high, right_high, dims) + (middle + small)


def triangle(width):
    tiles = width // LANES
    return [(i, j) for i in range(tiles) for j in range(i + 1)]


def column_of(row):
    return jnp.broadcast_to(row, (LANES, LANES)).T


def offset_of(me, levels):
    return sum(((me >> bit) & (members - 1)) * size for bit, members, size in levels)


def eye(size):
    return lax.broadcasted_iota(jnp.int32, (size, size), 0) == lax.broadcasted_iota(
        jnp.int32, (size, size), 1
    )


def code_floats(value):
    size = jnp.abs(value.astype(F32))
    power = jnp.floor(jnp.log2(jnp.maximum(size, 2.0**-126)))
    mantissa = size * jnp.exp2(-power)
    power = power + jnp.where(mantissa >= 2.0, 1.0, 0.0) - jnp.where(mantissa < 1.0, 1.0, 0.0)
    mantissa = jnp.where(
        mantissa >= 2.0, mantissa * 0.5, jnp.where(mantissa < 1.0, mantissa * 2.0, mantissa)
    )
    code = (power + 127.0) * 128.0 + jnp.round((mantissa - 1.0) * 128.0)
    code = jnp.where(size < 2.0**-126, 0.0, code)
    return jnp.where(value.astype(F32) < 0.0, -code, code)


def float_of(code):
    size = jnp.abs(code)
    power = lax.shift_right_logical(size, 7).astype(F32) - 127.0
    value = (1.0 + (size & 127).astype(F32) / 128.0) * jnp.exp2(power)
    value = jnp.where(size == 0, 0.0, value)
    return jnp.where(code < 0, -value, value)


def decode(codes_ref, scale_ref, start, target_ref):
    rows, width = target_ref.shape
    for g in range(rows // LANES):
        index = scale_ref[pl.ds(start // LANES + g, 1), :]
        scale = column_of(jnp.exp2(index.astype(F32) / 16.0) / 128.0)
        at = pl.multiple_of(start + g * LANES, LANES)
        for c in range(width // LANES):
            cols = slice(c * LANES, (c + 1) * LANES)
            value = codes_ref[pl.ds(at, LANES), cols].astype(F32) * scale
            target_ref[g * LANES : (g + 1) * LANES, cols] = value.astype(BF16)


def gram_kernel(
    weight_store,
    weight_new,
    me_ref,
    lengths_ref,
    scale_ref,
    queries_ref,
    act_hbm,
    grad_hbm,
    basis_in_hbm,
    basis_out_hbm,
    codes_hbm,
    new_rows_ref,
    keep_ref,
    send_ref,
    diag_ref,
    asked_ref,
    act,
    grad,
    basis_in,
    basis_out,
    codes,
    stored,
    stored_next,
    total,
    sems,
    code_sems,
):
    rows, width = codes.shape
    rank = basis_in.shape[0]
    tokens = act.shape[0]
    examples = new_rows_ref.shape[0]
    chunk = stored.shape[0]
    cuts = 4
    span = grad.shape[1] // cuts
    parts = [(basis_out_hbm, basis_out)]
    for c in range(cuts):
        at = (slice(None), slice(c * span, (c + 1) * span))
        parts.append((grad_hbm.at[at], grad.at[at]))
    parts += [(basis_in_hbm, basis_in), (act_hbm, act)]
    copies = [
        pltpu.make_async_copy(source, target, sems.at[i])
        for i, (source, target) in enumerate(parts)
    ]

    def code_copy(c):
        at = pl.ds(pl.multiple_of(c * chunk, chunk), chunk)
        return pltpu.make_async_copy(codes_hbm.at[at, :], codes.at[at, :], code_sems.at[c])

    chunks = rows // chunk
    for c in range(chunks // 2):
        code_copy(c).start()
    for copy in copies:
        copy.start()
    for c in range(chunks // 2, chunks):
        code_copy(c).start()
    asked = code_floats(queries_ref[...])
    asked = [asked[:, i * LANES : (i + 1) * LANES] for i in range(width // LANES)]
    asked_ref[...] = jnp.concatenate(asked, axis=0).astype(jnp.int32).astype(jnp.int16)
    side = 256

    def ready(c, target):
        code_copy(c).wait()
        decode(codes, scale_ref, c * chunk, target)

    def add(source, first):
        for i in range(width // side):
            at = slice(i * side, (i + 1) * side)
            to = slice(0, (i + 1) * side)
            value = mm(source[:, at], source[:, to], TN)
            total[at, to] = value if first else total[at, to] + value

    ready(0, stored)
    ready(1, stored_next)
    add(stored, True)

    def body(pair, _):
        ready(2 * pair + 2, stored)
        add(stored_next, False)
        ready(2 * pair + 3, stored_next)
        add(stored, False)
        return 0

    lax.fori_loop(0, chunks // 4 - 1, body, 0)
    copies[0].wait()
    proj_out = jnp.zeros((tokens, rank), F32)
    for c in range(cuts):
        copies[1 + c].wait()
        at = (slice(None), slice(c * span, (c + 1) * span))
        proj_out = proj_out + mm(grad[at], basis_out[at], NT)
    copies[-2].wait()
    copies[-1].wait()
    proj_in = mm(act[...], basis_in[...], NT)
    wide = (3 * rank, width)
    k = lax.broadcasted_iota(jnp.int32, wide, 0) & (rank - 1)
    c = lax.broadcasted_iota(jnp.int32, wide, 1)
    pick_in = (k == lax.shift_right_logical(c, rank.bit_length() - 1)).astype(F32).astype(BF16)
    pick_out = (k == (c & (rank - 1))).astype(F32).astype(BF16)
    left = mm(jnp.concatenate(split3(proj_in), axis=1), pick_in)
    right = mm(jnp.concatenate(split3(proj_out), axis=1), pick_out)
    products = split3(left * right)
    place = lax.broadcasted_iota(jnp.int32, (examples, tokens), 1)
    owner = lax.broadcasted_iota(jnp.int32, (examples, tokens), 0)
    member = jnp.zeros((examples, tokens), F32)
    start = jnp.int32(0)
    for e in range(examples):
        finish = start + lengths_ref[0, e]
        inside = (owner == e) & (place >= start) & (place < finish)
        member = jnp.where(inside, 1.0, member)
        start = finish
    member = member.astype(BF16)
    new_rows = mm(member, products[0]) + (mm(member, products[1]) + mm(member, products[2]))
    new_rows_ref[...] = new_rows
    high, mid, low = [part.astype(F32) for part in split3(new_rows)]
    first = jnp.concatenate([high, high, mid, high, low, mid], axis=0).astype(BF16)
    second = jnp.concatenate([high, mid, high, low, high, mid], axis=0).astype(BF16)
    lax.fori_loop(chunks // 4 - 1, chunks // 2 - 1, body, 0)
    add(stored_next, False)
    tiles = triangle(width)
    half = len(tiles) // 2
    diagonal = eye(LANES)

    def finish(mine):
        for i in range(width // side):
            for j in range(i + 1):
                down = slice(i * side, (i + 1) * side)
                across = slice(j * side, (j + 1) * side)
                value = weight_store * total[down, across] + weight_new * mm(
                    first[:, down], second[:, across], TN
                )
                for b, (p, q) in enumerate(tiles):
                    if p // 2 != i or q // 2 != j:
                        continue
                    tile = value[
                        p % 2 * LANES : (p % 2 + 1) * LANES, q % 2 * LANES : (q % 2 + 1) * LANES
                    ]
                    target = keep_ref if b // half == mine else send_ref
                    target[b % half * LANES : (b % half + 1) * LANES, :] = tile
                    if p == q:
                        diag_ref[p : p + 1, :] = jnp.sum(
                            jnp.where(diagonal, tile, 0.0), axis=0, keepdims=True
                        )

    for mine in range(2):
        pl.when((me_ref[0] & 1) == mine)(functools.partial(finish, mine))
    send_ref[half * LANES :, :] = diag_ref[...]


def gram(
    me, lengths, codes, scale_index, queries, activations, out_grads, basis_in, basis_out, count
):
    rows, width = codes.shape
    examples = lengths.shape[1]
    half = len(triangle(width)) // 2 * LANES
    chunk = 256
    extra = width // LANES
    return pl.pallas_call(
        functools.partial(gram_kernel, 0.75 / (count * rows), 0.25 / (count * examples)),
        in_specs=[SMEM, SMEM, VMEM, VMEM] + [ANY] * 5,
        out_specs=[VMEM] * 5,
        out_shape=[
            jax.ShapeDtypeStruct((examples, width), F32),
            jax.ShapeDtypeStruct((half, LANES), F32),
            jax.ShapeDtypeStruct((half + extra, LANES), F32),
            jax.ShapeDtypeStruct((extra, LANES), F32),
            jax.ShapeDtypeStruct((queries.shape[0] * extra, LANES), jnp.int16),
        ],
        scratch_shapes=[
            pltpu.VMEM(activations.shape, BF16),
            pltpu.VMEM(out_grads.shape, BF16),
            pltpu.VMEM(basis_in.shape, BF16),
            pltpu.VMEM(basis_out.shape, BF16),
            pltpu.VMEM((rows, width), jnp.int32),
            pltpu.VMEM((chunk, width), BF16),
            pltpu.VMEM((chunk, width), BF16),
            pltpu.VMEM((width, width), F32),
            pltpu.SemaphoreType.DMA((8,)),
            pltpu.SemaphoreType.DMA((rows // chunk,)),
        ],
        compiler_params=pltpu.CompilerParams(vmem_limit_bytes=57 << 20),
        cost_estimate=pl.CostEstimate(
            flops=6 * 10**9, bytes_accessed=30 * 10**6, transcendentals=0
        ),
        name="fisher_share",
    )(
        me,
        lengths,
        scale_index,
        queries,
        activations,
        out_grads,
        basis_in,
        basis_out,
        codes,
    )


def exponents(diag):
    return jnp.clip(jnp.ceil(32.0 * jnp.log2(jnp.maximum(diag, 1e-30))), -4000.0, 4000.0)


def fill_scales(exps, factor, columns, rows_ref):
    scale = jnp.exp2(exps / 64.0)
    rows_ref[...] = scale * factor
    for t in range(exps.shape[0]):
        columns[t * LANES : (t + 1) * LANES, :] = column_of(scale[t : t + 1, :])


def read_exps(ref, start, tiles):
    return ref[start : start + PACK, :].astype(jnp.int32).astype(F32)[:tiles, :]


def write_exps(ref, start, exps):
    tiles = exps.shape[0]
    padded = jnp.concatenate([exps, jnp.zeros((PACK - tiles, LANES), F32)], axis=0)
    ref[start : start + PACK, :] = padded.astype(jnp.int32).astype(jnp.int16)


def encode(value, inverse):
    scaled = jnp.clip(jnp.round(value * inverse), -CODE_MAX, CODE_MAX)
    return scaled.astype(jnp.int32).astype(jnp.int16)


def strip_scale(table_ref, columns, rows_ref, flat, strip):
    tile = flat // LANES
    i = table_ref[0, tile]
    j = table_ref[1, tile]
    at = pl.multiple_of(i * LANES + flat % LANES, strip)
    return columns[pl.ds(at, strip), :] * rows_ref[pl.ds(j, 1), :]


def fetch_kernel(first_hbm, second_hbm, first_ref, second_ref, sems):
    copies = [pltpu.make_async_copy(second_hbm, second_ref, sems.at[0])]
    rows = first_ref.shape[0] // 4
    for c in range(4):
        at = pl.ds(c * rows, rows)
        copies.append(
            pltpu.make_async_copy(first_hbm.at[at, :], first_ref.at[at, :], sems.at[c + 1])
        )
    for copy in copies:
        copy.start()
    for copy in copies:
        copy.wait()


def fetch_rows(first, second):
    return pl.pallas_call(
        fetch_kernel,
        in_specs=[ANY, ANY],
        out_specs=[VMEM, VMEM],
        out_shape=[
            jax.ShapeDtypeStruct(first.shape, first.dtype),
            jax.ShapeDtypeStruct(second.shape, second.dtype),
        ],
        scratch_shapes=[pltpu.SemaphoreType.DMA((5,))],
        compiler_params=pltpu.CompilerParams(vmem_limit_bytes=32 << 20),
        cost_estimate=pl.CostEstimate(
            flops=0, bytes_accessed=2 * first.size * first.dtype.itemsize, transcendentals=0
        ),
        name="fetch_rows",
    )(first, second)


def combine_kernel(levels, bit, members, has_own, coded, tiles, strip, *refs):
    me_ref, table_ref = refs[:2]
    refs = refs[2:]
    if has_own:
        (own_ref, state_ref), refs = refs[:2], refs[2:]
    arrived, refs = refs[:coded], refs[coded:]
    if members < 2:
        asked_ref, refs = refs[0], refs[1:]
    if members > 1:
        (out_own, out_state), refs = refs[:2], refs[2:]
        targets, refs = refs[: members - 1], refs[members - 1 :]
    else:
        (out_own, out_state), refs = refs[:2], refs[2:]
        targets = [out_own]
    columns, rows_ref, inverse_columns, inverse_rows = refs
    extra = asked_ref.shape[0] if members < 2 else 0
    rows = (out_own.shape[0] - (PACK if members else 0) - extra) if members < 2 else (
        own_ref.shape[0]
    )
    if not members and not has_own:
        rows = out_own.shape[0] - 2 * extra
    if arrived[0].dtype == F32:
        exps = exponents(state_ref[...] + arrived[0][rows:, :])
    else:
        theirs = [read_exps(ref, rows, tiles) for ref in arrived]
        known = [read_exps(state_ref, 0, tiles)] if has_own else []
        level = [jnp.exp2(e / 32.0) for e in known + theirs]
        while len(level) > 1:
            level = [a + b for a, b in zip(level[::2], level[1::2])]
        exps = exponents(level[0])
        for m, e in enumerate(theirs):
            fill_scales(e, 1.0 / CODE_MAX, columns.at[m], rows_ref.at[m])
    fill_scales(-exps, CODE_MAX, inverse_columns, inverse_rows)
    base = offset_of(me_ref[0], levels)
    mine_at = (me_ref[0] >> bit) & (members - 1) if members > 1 else 0
    part = rows // max(members, 1)
    for m in range(max(members, 1)):
        first = (mine_at ^ m) * part

        def body(s, _):
            inside = pl.multiple_of(s * strip, strip)
            at = pl.multiple_of(first + inside, strip)
            flat = base + at
            value = own_ref[pl.ds(at, strip), :] if has_own else 0.0
            for a, ref in enumerate(arrived):
                got = ref[pl.ds(at, strip), :]
                if got.dtype == F32:
                    value = value + got
                else:
                    got = got.astype(jnp.int32).astype(F32)
                    value = value + got * strip_scale(
                        table_ref, columns.at[a], rows_ref.at[a], flat, strip
                    )
            if members > 1 and m == 0:
                out_own[pl.ds(inside, strip), :] = value
            else:
                inverse = strip_scale(table_ref, inverse_columns, inverse_rows, flat, strip)
                target = targets[max(m - 1, 0)]
                target[pl.ds(inside, strip), :] = encode(value, inverse)
            return 0

        lax.fori_loop(0, part // strip, body, 0, unroll=9)
    write_exps(out_state, 0, exps)
    if members:
        for ref in targets:
            write_exps(ref, part, exps)
    if members == 1:
        out_own[rows + PACK :, :] = asked_ref[...]
    elif not members and has_own:
        out_own[rows:, :] = asked_ref[...]
    elif not members:
        out_own[rows : rows + extra, :] = asked_ref[...]
        out_own[rows + extra :, :] = arrived[1][rows + PACK :, :]


def combine(me, table, levels, rows, own, arrived, bit, members, strip, asked):
    tiles = table.shape[1]
    width_tiles = int(round(((8 * tiles + 1) ** 0.5 - 1) / 2))
    width = width_tiles * LANES
    part = rows // max(members, 1)
    short = jnp.int16
    state = jax.ShapeDtypeStruct((PACK, LANES), short)
    if members > 1:
        message = jax.ShapeDtypeStruct((part + PACK, LANES), short)
        outs = [jax.ShapeDtypeStruct((part, LANES), F32), state] + [message] * (members - 1)
        more = []
    else:
        extra = asked.shape[0]
        size = rows + (PACK + extra if members else extra if own else 2 * extra)
        outs = [jax.ShapeDtypeStruct((size, LANES), short), state]
        more = [asked]
    operands = [*own, *arrived, *more]
    return pl.pallas_call(
        functools.partial(
            combine_kernel,
            levels,
            bit,
            members,
            bool(own),
            len(arrived),
            width_tiles,
            strip,
        ),
        in_specs=[SMEM, SMEM] + [VMEM] * len(operands),
        out_specs=[VMEM] * len(outs),
        out_shape=outs,
        scratch_shapes=[
            pltpu.VMEM((len(arrived), width, LANES), F32),
            pltpu.VMEM((len(arrived), width_tiles, LANES), F32),
            pltpu.VMEM((width, LANES), F32),
            pltpu.VMEM((width_tiles, LANES), F32),
        ],
        compiler_params=pltpu.CompilerParams(vmem_limit_bytes=32 << 20),
        cost_estimate=pl.CostEstimate(
            flops=10 * rows * LANES, bytes_accessed=8 * rows * LANES, transcendentals=0
        ),
        name="sum_shares",
    )(me, table, *operands)


def solve_kernel(
    side,
    levels,
    masks,
    count,
    slot_bits,
    me_ref,
    first_ref,
    second_ref,
    state_ref,
    new_rows_ref,
    scale_ref,
    codes_hbm,
    scores_hbm,
    new_scores_ref,
    flat,
    system,
    pair,
    stored,
    solved,
    columns,
    rows_ref,
    codes,
    scores,
    taken_ref,
    sems,
    out_sems,
):
    lots = sems.shape[0]
    lot = codes.shape[0] // lots

    def fetch(c):
        at = pl.ds(pl.multiple_of(c * lot, lot), lot)
        return pltpu.make_async_copy(codes_hbm.at[at, :], codes.at[at, :], sems.at[c])

    for c in range(lots):
        fetch(c).start()
    queries, width = solved.shape
    tiles = width // LANES
    pieces = len(masks)
    piece = flat.shape[0] // pieces
    pitch = 2 * first_ref.shape[0] // pieces
    asked = []
    for p in range(pieces):
        source = first_ref if p < pieces // 2 else second_ref
        at = p % (pieces // 2) * pitch
        place = pl.multiple_of(offset_of(me_ref[0] ^ masks[p], levels), PACK)
        flat[pl.ds(place, piece), :] = source[at : at + piece, :]
        asked.append(source[at + piece : at + pitch, :].astype(jnp.int32))
    asked = float_of(jnp.concatenate(asked, axis=0)).astype(BF16)
    each = queries // count
    packet = each * tiles
    order = (tiles * queries, asked.shape[0])
    to = lax.broadcasted_iota(jnp.int32, order, 0)
    source = lax.broadcasted_iota(jnp.int32, order, 1)
    slot = lax.shift_right_logical(source, packet.bit_length() - 1)
    owner = jnp.zeros(order, jnp.int32)
    for bit, position in enumerate(slot_bits):
        owner = owner | ((lax.shift_right_logical(slot, position) & 1) << bit)
    owner = owner ^ me_ref[0]
    inside = source & (packet - 1)
    target = (
        lax.shift_right_logical(inside, each.bit_length() - 1) * queries
        + owner * each
        + (inside & (each - 1))
    )
    asked = mm((target == to).astype(F32).astype(BF16), asked)
    for i in range(tiles):
        system[width:, i * LANES : (i + 1) * LANES] = asked[i * queries : (i + 1) * queries, :]
    fill_scales(read_exps(state_ref, 0, tiles), 1.0 / CODE_MAX, columns, rows_ref)
    diagonal = eye(LANES)
    trace = jnp.zeros((1, LANES), F32)
    for b, (i, j) in enumerate(triangle(width)):
        value = flat[b * LANES : (b + 1) * LANES, :].astype(jnp.int32).astype(F32)
        value = value * columns[i * LANES : (i + 1) * LANES, :] * rows_ref[j : j + 1, :]
        system[i * LANES : (i + 1) * LANES, j * LANES : (j + 1) * LANES] = value
        if i == j:
            trace = trace + jnp.sum(jnp.where(diagonal, value, 0.0), axis=0, keepdims=True)
        elif i * LANES // side == j * LANES // side:
            system[j * LANES : (j + 1) * LANES, i * LANES : (i + 1) * LANES] = value.T
    damp = (0.1 / width) * jnp.sum(trace)
    for i in range(tiles):
        at = slice(i * LANES, (i + 1) * LANES)
        system[at, at] += jnp.where(diagonal, damp, 0.0)
    blocks = width // side
    spans = [slice(b * side, (b + 1) * side) for b in range(blocks)]
    unit = eye(side)
    def await_lot(c):
        @pl.when(c < lots)
        def _():
            fetch(c).wait()

    def decode_lot(c):
        start = pl.multiple_of(jnp.minimum(c, lots - 1) * lot, lot)
        decode(codes, scale_ref, start, stored.at[pl.ds(start, lot), :])

    def eliminate(split, mul, refine):
        for b, span in enumerate(spans):
            below = (b + 1) * side
            block = system[span, span]
            bound = jnp.max(jnp.sum(jnp.abs(block), axis=0, keepdims=True))
            low = damp / bound

            def step_from(value, low):
                gain = 4.0 / ((1.0 + low) * (1.0 + low))
                return gain, jnp.where(unit, gain * (1.0 + low), 0.0) - gain * value

            block = block * (1.0 / bound)
            gain, step = step_from(block, low)
            pair[:side, :] = step * (1.0 / bound)
            pair[side:, :] = mul(split(block), split(step))

            def more(low):
                return low < 0.95

            def newton(low):
                taken = taken_ref[0]
                taken_ref[0] = taken + 1
                await_lot(taken)
                both = pair[...]
                gain, step = step_from(both[side:, :], low)
                decode_lot(taken)
                pair[...] = mul(split(both), split(step))
                return gain * low

            low = lax.while_loop(more, newton, gain * low)
            both = pair[...]
            gain, step = step_from(both[side:, :], low)
            low = gain * low
            inverse = mul(split(both[:side, :]), split(step)) * (2.0 / (1.0 + low))
            if refine:
                left = jnp.where(unit, 1.0, 0.0) - mul(split(system[span, span]), split(inverse))
                inverse = inverse + mul(split(inverse), split(left))
            inverse = split(inverse)
            panel = system[below:, span]
            weights = split(mul(split(panel), inverse))
            later = split(panel[: width - below, :])
            system[below:, span] = sum(part.astype(F32) for part in weights)
            for c in range(b + 1, blocks):
                from_row = c * side - below
                update = mul(
                    tuple(part[from_row:, :] for part in weights),
                    tuple(part[from_row : from_row + side, :] for part in later),
                    NT,
                )
                system[c * side :, spans[c]] -= update
        for b in reversed(range(blocks)):
            below = (b + 1) * side
            value = system[width:, spans[b]]
            if below < width:
                value = value - mul(
                    split(solved[:, below:]), split(system[below:width, spans[b]])
                )
            solved[:, spans[b]] = value

    taken_ref[0] = 0
    ratio = jnp.float32(0.0)
    for span in spans:
        sums = jnp.sum(jnp.abs(system[span, span]), axis=0, keepdims=True)
        ratio = jnp.maximum(ratio, jnp.max(sums) / damp)
    pl.when(ratio <= 800.0)(lambda: eliminate(split2, mm3, False))
    pl.when(jnp.logical_not(ratio <= 800.0))(lambda: eliminate(split3, mm6, True))
    high, low = split2(solved[...])
    new_scores_ref[...] = mm3(split2(new_rows_ref[...]), (high, low), NT)
    both = jnp.concatenate([high, low], axis=0)

    def rest(c, _):
        fetch(c).wait()
        decode_lot(c)
        return 0

    lax.fori_loop(jnp.minimum(taken_ref[0], lots), lots, rest, 0)
    span = scores.shape[1] // out_sems.shape[0]
    copies = []
    for c in range(out_sems.shape[0]):
        at = slice(c * span, (c + 1) * span)
        value = mm(both, stored[at, :], NT)
        scores[:, at] = value[:queries, :] + value[queries:, :]
        out = pltpu.make_async_copy(scores.at[:, at], scores_hbm.at[:, at], out_sems.at[c])
        out.start()
        copies.append(out)
    for out in copies:
        out.wait()


def solve(
    me, levels, masks, count, slot_bits, first, second, state, new_rows, scale_index, codes, asked
):
    rows, width = codes.shape
    examples = new_rows.shape[0]
    side = 256
    flat_rows = len(triangle(width)) * LANES
    return pl.pallas_call(
        functools.partial(solve_kernel, side, levels, masks, count, slot_bits),
        in_specs=[SMEM] + [VMEM] * 5 + [ANY],
        out_specs=[ANY, VMEM],
        out_shape=[
            jax.ShapeDtypeStruct((asked, rows), F32),
            jax.ShapeDtypeStruct((examples, asked), F32),
        ],
        scratch_shapes=[
            pltpu.VMEM((flat_rows, LANES), jnp.int16),
            pltpu.VMEM((width + asked, width), F32),
            pltpu.VMEM((2 * side, side), F32),
            pltpu.VMEM((rows, width), BF16),
            pltpu.VMEM((asked, width), F32),
            pltpu.VMEM((width, LANES), F32),
            pltpu.VMEM((width // LANES, LANES), F32),
            pltpu.VMEM((rows, width), jnp.int32),
            pltpu.VMEM((asked, rows), F32),
            pltpu.SMEM((1,), jnp.int32),
            pltpu.SemaphoreType.DMA((rows // (2 * LANES),)),
            pltpu.SemaphoreType.DMA((8,)),
        ],
        compiler_params=pltpu.CompilerParams(vmem_limit_bytes=46 << 20),
        cost_estimate=pl.CostEstimate(
            flops=10 * 10**9, bytes_accessed=20 * 10**6, transcendentals=0
        ),
        name="solve_and_score",
    )(me, first, second, state, new_rows, scale_index, codes)


def swap(value, mask, count):
    return lax.ppermute(value, "store", [(i, i ^ mask) for i in range(count)])


def shards(activations, out_grads, basis_in, basis_out, lengths, codes, scale_index, queries):
    count = lax.axis_size("store")
    me = lax.axis_index("store").astype(jnp.int32)[None]
    width = codes.shape[1]
    tiles = triangle(width)
    table = np.array(tiles, np.int32).T
    scale_index = scale_index.reshape(-1, LANES)
    new_rows, own, send, state, asked = gram(
        me,
        lengths,
        codes,
        scale_index,
        queries,
        activations,
        out_grads,
        basis_in,
        basis_out,
        count,
    )
    groups = []
    bit = 1
    while 1 << bit < count:
        members = 4 if 1 << (bit + 1) < count else 2
        groups.append((bit, members))
        bit += 2
    piece = len(tiles) * LANES // 2
    for _, members in groups:
        piece //= members if members > 2 else 1
    strip = int(np.gcd(np.gcd(piece, LANES), 64))
    arrived = [swap(send, 1, count)]
    rows = own.shape[0]
    levels = [(0, 2, rows)]
    own = fetch_rows(own, state)
    for bit, members in groups:
        if members == 2:
            coded, _ = combine(me, table, levels, rows, own, arrived, bit, 1, strip, asked)
            own, arrived = [], [coded, swap(coded, 1 << bit, count)]
            break
        own = combine(me, table, levels, rows, own, arrived, bit, members, strip, asked)
        own, messages = own[:2], own[2:]
        arrived = [swap(message, (m + 1) << bit, count) for m, message in enumerate(messages)]
        rows //= members
        levels = levels + [(bit, members, rows)]
    final, state = combine(me, table, levels, rows, own, arrived, 0, 0, strip, asked)
    for bit, members in reversed(groups):
        if members > 2:
            final = jnp.concatenate(
                [final] + [swap(final, m << bit, count) for m in range(1, members)], axis=0
            )
    other = swap(final, 1, count)
    slot_bits = [count.bit_length() - 2]
    for bit, members in groups:
        for low in range(members // 2):
            slot_bits.append(slot_bits[0] - (bit + members // 2 - 1) + low)
    packets = len(tiles) * LANES // rows
    masks = []
    for slot in range(packets):
        first = slot * (count // packets)
        masks.append(sum((first >> position & 1) << b for b, position in enumerate(slot_bits)))
    scores, new_scores = solve(
        me,
        levels,
        masks,
        count,
        slot_bits,
        final,
        other,
        state,
        new_rows,
        scale_index,
        codes,
        count * queries.shape[0],
    )
    return new_rows, scores, new_scores.T


def solution(mesh):
    return jax.shard_map(
        shards,
        mesh=mesh,
        in_specs=(
            P(("groups", "store"), None),
            P(("groups", "store"), None),
            P(),
            P(),
            P(("groups", "store"), None),
            P(("groups", "store"), None),
            P(("groups", "store")),
            P(("groups", "store"), None),
        ),
        out_specs=(P(("groups", "store"), None), P("groups", "store"), P("groups", "store")),
        check_vma=False,
    )
```

```python
import functools

import jax
import jax.numpy as jnp
import numpy as np
from jax import lax
from jax.experimental import pallas as pl
from jax.experimental.pallas import tpu as pltpu
from jax.sharding import PartitionSpec as P

LANES = 128
PACK = 16
CODE_MAX = 32767.0
F32 = jnp.float32
BF16 = jnp.bfloat16
VMEM = pl.BlockSpec(memory_space=pltpu.VMEM)
SMEM = pl.BlockSpec(memory_space=pltpu.SMEM)
ANY = pl.BlockSpec(memory_space=pl.ANY)
NN = (((1,), (0,)), ((), ()))
NT = (((1,), (1,)), ((), ()))
TN = (((0,), (0,)), ((), ()))


def mm(left, right, dims=NN):
    return lax.dot_general(left, right, dims, preferred_element_type=F32)


def split2(value):
    high = value.astype(BF16)
    return high, (value - high.astype(F32)).astype(BF16)


def split3(value):
    high, _ = split2(value)
    rest = value - high.astype(F32)
    mid, low = split2(rest)
    return high, mid, low


def mm3(left, right, dims=NN):
    left_high, left_low = left
    right_high, right_low = right
    return mm(left_high, right_high, dims) + (
        mm(left_high, right_low, dims) + mm(left_low, right_high, dims)
    )


def mm6(left, right, dims=NN):
    left_high, left_mid, left_low = left
    right_high, right_mid, right_low = right
    small = mm(left_high, right_low, dims) + mm(left_low, right_high, dims)
    small = small + mm(left_mid, right_mid, dims)
    middle = mm(left_high, right_mid, dims) + mm(left_mid, right_high, dims)
    return mm(left_high, right_high, dims) + (middle + small)


def triangle(width):
    tiles = width // LANES
    return [(i, j) for i in range(tiles) for j in range(i + 1)]


def column_of(row):
    return jnp.broadcast_to(row, (LANES, LANES)).T


def offset_of(me, levels):
    return sum(((me >> bit) & (members - 1)) * size for bit, members, size in levels)


def eye(size):
    return lax.broadcasted_iota(jnp.int32, (size, size), 0) == lax.broadcasted_iota(
        jnp.int32, (size, size), 1
    )


def code_floats(value):
    size = jnp.abs(value.astype(F32))
    power = jnp.floor(jnp.log2(jnp.maximum(size, 2.0**-126)))
    mantissa = size * jnp.exp2(-power)
    power = power + jnp.where(mantissa >= 2.0, 1.0, 0.0) - jnp.where(mantissa < 1.0, 1.0, 0.0)
    mantissa = jnp.where(
        mantissa >= 2.0, mantissa * 0.5, jnp.where(mantissa < 1.0, mantissa * 2.0, mantissa)
    )
    code = (power + 127.0) * 128.0 + jnp.round((mantissa - 1.0) * 128.0)
    code = jnp.where(size < 2.0**-126, 0.0, code)
    return jnp.where(value.astype(F32) < 0.0, -code, code)


def float_of(code):
    size = jnp.abs(code)
    power = lax.shift_right_logical(size, 7).astype(F32) - 127.0
    value = (1.0 + (size & 127).astype(F32) / 128.0) * jnp.exp2(power)
    value = jnp.where(size == 0, 0.0, value)
    return jnp.where(code < 0, -value, value)


def decode(codes_ref, scale_ref, start, target_ref):
    rows, width = target_ref.shape
    for g in range(rows // LANES):
        index = scale_ref[pl.ds(start // LANES + g, 1), :]
        scale = column_of(jnp.exp2(index.astype(F32) / 16.0) / 128.0)
        at = pl.multiple_of(start + g * LANES, LANES)
        for c in range(width // LANES):
            cols = slice(c * LANES, (c + 1) * LANES)
            value = codes_ref[pl.ds(at, LANES), cols].astype(F32) * scale
            target_ref[g * LANES : (g + 1) * LANES, cols] = value.astype(BF16)


def gram_kernel(
    weight_store,
    weight_new,
    me_ref,
    lengths_ref,
    scale_ref,
    queries_ref,
    act_hbm,
    grad_hbm,
    basis_in_hbm,
    basis_out_hbm,
    codes_hbm,
    new_rows_ref,
    keep_ref,
    send_ref,
    diag_ref,
    asked_ref,
    act,
    grad,
    basis_in,
    basis_out,
    codes,
    stored,
    stored_next,
    total,
    sems,
    code_sems,
):
    rows, width = codes.shape
    rank = basis_in.shape[0]
    tokens = act.shape[0]
    examples = new_rows_ref.shape[0]
    chunk = stored.shape[0]
    cuts = 4
    span = grad.shape[1] // cuts
    parts = [(basis_in_hbm, basis_in), (act_hbm, act), (basis_out_hbm, basis_out)]
    for c in range(cuts):
        at = (slice(None), slice(c * span, (c + 1) * span))
        parts.append((grad_hbm.at[at], grad.at[at]))
    copies = [
        pltpu.make_async_copy(source, target, sems.at[i])
        for i, (source, target) in enumerate(parts)
    ]

    def code_copy(c):
        at = pl.ds(pl.multiple_of(c * chunk, chunk), chunk)
        return pltpu.make_async_copy(codes_hbm.at[at, :], codes.at[at, :], code_sems.at[c])

    chunks = rows // chunk
    early = 2 * (5 * chunks // 16)
    for c in range(early):
        code_copy(c).start()
    for copy in copies:
        copy.start()
    for c in range(early, chunks):
        code_copy(c).start()
    asked = code_floats(queries_ref[...])
    asked = [asked[:, i * LANES : (i + 1) * LANES] for i in range(width // LANES)]
    asked_ref[...] = jnp.concatenate(asked, axis=0).astype(jnp.int32).astype(jnp.int16)
    side = 256

    def ready(c, target):
        code_copy(c).wait()
        decode(codes, scale_ref, c * chunk, target)

    def add(source, first):
        for i in range(width // side):
            at = slice(i * side, (i + 1) * side)
            to = slice(0, (i + 1) * side)
            value = mm(source[:, at], source[:, to], TN)
            total[at, to] = value if first else total[at, to] + value

    ready(0, stored)
    ready(1, stored_next)
    add(stored, True)

    def body(pair, _):
        ready(2 * pair + 2, stored)
        add(stored_next, False)
        ready(2 * pair + 3, stored_next)
        add(stored, False)
        return 0

    lax.fori_loop(0, early // 2 - 1, body, 0)
    copies[0].wait()
    copies[1].wait()
    proj_in = mm(act[...], basis_in[...], NT)
    copies[2].wait()
    proj_out = jnp.zeros((tokens, rank), F32)
    for c in range(cuts):
        copies[3 + c].wait()
        at = (slice(None), slice(c * span, (c + 1) * span))
        proj_out = proj_out + mm(grad[at], basis_out[at], NT)
    wide = (3 * rank, width)
    k = lax.broadcasted_iota(jnp.int32, wide, 0) & (rank - 1)
    c = lax.broadcasted_iota(jnp.int32, wide, 1)
    pick_in = (k == lax.shift_right_logical(c, rank.bit_length() - 1)).astype(F32).astype(BF16)
    pick_out = (k == (c & (rank - 1))).astype(F32).astype(BF16)
    left = mm(jnp.concatenate(split3(proj_in), axis=1), pick_in)
    right = mm(jnp.concatenate(split3(proj_out), axis=1), pick_out)
    products = split3(left * right)
    place = lax.broadcasted_iota(jnp.int32, (examples, tokens), 1)
    owner = lax.broadcasted_iota(jnp.int32, (examples, tokens), 0)
    member = jnp.zeros((examples, tokens), F32)
    start = jnp.int32(0)
    for e in range(examples):
        finish = start + lengths_ref[0, e]
        inside = (owner == e) & (place >= start) & (place < finish)
        member = jnp.where(inside, 1.0, member)
        start = finish
    member = member.astype(BF16)
    new_rows = mm(member, products[0]) + (mm(member, products[1]) + mm(member, products[2]))
    new_rows_ref[...] = new_rows
    high, mid, low = [part.astype(F32) for part in split3(new_rows)]
    first = jnp.concatenate([high, high, mid, high, low, mid], axis=0).astype(BF16)
    second = jnp.concatenate([high, mid, high, low, high, mid], axis=0).astype(BF16)
    lax.fori_loop(early // 2 - 1, chunks // 2 - 1, body, 0)
    add(stored_next, False)
    tiles = triangle(width)
    half = len(tiles) // 2
    diagonal = eye(LANES)

    def finish(mine):
        for i in range(width // side):
            for j in range(i + 1):
                down = slice(i * side, (i + 1) * side)
                across = slice(j * side, (j + 1) * side)
                value = weight_store * total[down, across] + weight_new * mm(
                    first[:, down], second[:, across], TN
                )
                for b, (p, q) in enumerate(tiles):
                    if p // 2 != i or q // 2 != j:
                        continue
                    tile = value[
                        p % 2 * LANES : (p % 2 + 1) * LANES, q % 2 * LANES : (q % 2 + 1) * LANES
                    ]
                    target = keep_ref if b // half == mine else send_ref
                    target[b % half * LANES : (b % half + 1) * LANES, :] = tile
                    if p == q:
                        diag_ref[p : p + 1, :] = jnp.sum(
                            jnp.where(diagonal, tile, 0.0), axis=0, keepdims=True
                        )

    for mine in range(2):
        pl.when((me_ref[0] & 1) == mine)(functools.partial(finish, mine))
    send_ref[half * LANES :, :] = diag_ref[...]


def gram(
    me, lengths, codes, scale_index, queries, activations, out_grads, basis_in, basis_out, count
):
    rows, width = codes.shape
    examples = lengths.shape[1]
    half = len(triangle(width)) // 2 * LANES
    chunk = 256
    extra = width // LANES
    return pl.pallas_call(
        functools.partial(gram_kernel, 0.75 / (count * rows), 0.25 / (count * examples)),
        in_specs=[SMEM, SMEM, VMEM, VMEM] + [ANY] * 5,
        out_specs=[VMEM] * 5,
        out_shape=[
            jax.ShapeDtypeStruct((examples, width), F32),
            jax.ShapeDtypeStruct((half, LANES), F32),
            jax.ShapeDtypeStruct((half + extra, LANES), F32),
            jax.ShapeDtypeStruct((extra, LANES), F32),
            jax.ShapeDtypeStruct((queries.shape[0] * extra, LANES), jnp.int16),
        ],
        scratch_shapes=[
            pltpu.VMEM(activations.shape, BF16),
            pltpu.VMEM(out_grads.shape, BF16),
            pltpu.VMEM(basis_in.shape, BF16),
            pltpu.VMEM(basis_out.shape, BF16),
            pltpu.VMEM((rows, width), jnp.int32),
            pltpu.VMEM((chunk, width), BF16),
            pltpu.VMEM((chunk, width), BF16),
            pltpu.VMEM((width, width), F32),
            pltpu.SemaphoreType.DMA((8,)),
            pltpu.SemaphoreType.DMA((rows // chunk,)),
        ],
        compiler_params=pltpu.CompilerParams(vmem_limit_bytes=57 << 20),
        cost_estimate=pl.CostEstimate(
            flops=6 * 10**9, bytes_accessed=30 * 10**6, transcendentals=0
        ),
        name="fisher_share",
    )(
        me,
        lengths,
        scale_index,
        queries,
        activations,
        out_grads,
        basis_in,
        basis_out,
        codes,
    )


def exponents(diag):
    return jnp.clip(jnp.ceil(32.0 * jnp.log2(jnp.maximum(diag, 1e-30))), -4000.0, 4000.0)


def fill_scales(exps, factor, columns, rows_ref):
    scale = jnp.exp2(exps / 64.0)
    rows_ref[...] = scale * factor
    for t in range(exps.shape[0]):
        columns[t * LANES : (t + 1) * LANES, :] = column_of(scale[t : t + 1, :])


def read_exps(ref, start, tiles):
    return ref[start : start + PACK, :].astype(jnp.int32).astype(F32)[:tiles, :]


def write_exps(ref, start, exps):
    tiles = exps.shape[0]
    padded = jnp.concatenate([exps, jnp.zeros((PACK - tiles, LANES), F32)], axis=0)
    ref[start : start + PACK, :] = padded.astype(jnp.int32).astype(jnp.int16)


def encode(value, inverse):
    scaled = jnp.clip(jnp.round(value * inverse), -CODE_MAX, CODE_MAX)
    return scaled.astype(jnp.int32).astype(jnp.int16)


def strip_scale(table_ref, columns, rows_ref, flat, strip):
    tile = flat // LANES
    i = table_ref[0, tile]
    j = table_ref[1, tile]
    at = pl.multiple_of(i * LANES + flat % LANES, strip)
    return columns[pl.ds(at, strip), :] * rows_ref[pl.ds(j, 1), :]


def fetch_kernel(first_hbm, second_hbm, first_ref, second_ref, sems):
    copies = [pltpu.make_async_copy(second_hbm, second_ref, sems.at[0])]
    rows = first_ref.shape[0] // 4
    for c in range(4):
        at = pl.ds(c * rows, rows)
        copies.append(
            pltpu.make_async_copy(first_hbm.at[at, :], first_ref.at[at, :], sems.at[c + 1])
        )
    for copy in copies:
        copy.start()
    for copy in copies:
        copy.wait()


def fetch_rows(first, second):
    return pl.pallas_call(
        fetch_kernel,
        in_specs=[ANY, ANY],
        out_specs=[VMEM, VMEM],
        out_shape=[
            jax.ShapeDtypeStruct(first.shape, first.dtype),
            jax.ShapeDtypeStruct(second.shape, second.dtype),
        ],
        scratch_shapes=[pltpu.SemaphoreType.DMA((5,))],
        compiler_params=pltpu.CompilerParams(vmem_limit_bytes=32 << 20),
        cost_estimate=pl.CostEstimate(
            flops=0, bytes_accessed=2 * first.size * first.dtype.itemsize, transcendentals=0
        ),
        name="fetch_rows",
    )(first, second)


def combine_kernel(levels, bit, members, has_own, coded, tiles, strip, *refs):
    me_ref, table_ref = refs[:2]
    refs = refs[2:]
    if has_own:
        (own_ref, state_ref), refs = refs[:2], refs[2:]
    arrived, refs = refs[:coded], refs[coded:]
    if members < 2:
        asked_ref, refs = refs[0], refs[1:]
    if members > 1:
        (out_own, out_state), refs = refs[:2], refs[2:]
        targets, refs = refs[: members - 1], refs[members - 1 :]
    else:
        (out_own, out_state), refs = refs[:2], refs[2:]
        targets = [out_own]
    columns, rows_ref, inverse_columns, inverse_rows = refs
    extra = asked_ref.shape[0] if members < 2 else 0
    rows = (out_own.shape[0] - (PACK if members else 0) - extra) if members < 2 else (
        own_ref.shape[0]
    )
    if not members and not has_own:
        rows = out_own.shape[0] - 2 * extra
    if arrived[0].dtype == F32:
        exps = exponents(state_ref[...] + arrived[0][rows:, :])
    else:
        theirs = [read_exps(ref, rows, tiles) for ref in arrived]
        known = [read_exps(state_ref, 0, tiles)] if has_own else []
        level = [jnp.exp2(e / 32.0) for e in known + theirs]
        while len(level) > 1:
            level = [a + b for a, b in zip(level[::2], level[1::2])]
        exps = exponents(level[0])
        for m, e in enumerate(theirs):
            fill_scales(e, 1.0 / CODE_MAX, columns.at[m], rows_ref.at[m])
    fill_scales(-exps, CODE_MAX, inverse_columns, inverse_rows)
    base = offset_of(me_ref[0], levels)
    mine_at = (me_ref[0] >> bit) & (members - 1) if members > 1 else 0
    part = rows // max(members, 1)
    for m in range(max(members, 1)):
        first = (mine_at ^ m) * part

        def body(s, _):
            inside = pl.multiple_of(s * strip, strip)
            at = pl.multiple_of(first + inside, strip)
            flat = base + at
            value = own_ref[pl.ds(at, strip), :] if has_own else 0.0
            for a, ref in enumerate(arrived):
                got = ref[pl.ds(at, strip), :]
                if got.dtype == F32:
                    value = value + got
                else:
                    got = got.astype(jnp.int32).astype(F32)
                    value = value + got * strip_scale(
                        table_ref, columns.at[a], rows_ref.at[a], flat, strip
                    )
            if members > 1 and m == 0:
                out_own[pl.ds(inside, strip), :] = value
            else:
                inverse = strip_scale(table_ref, inverse_columns, inverse_rows, flat, strip)
                target = targets[max(m - 1, 0)]
                target[pl.ds(inside, strip), :] = encode(value, inverse)
            return 0

        lax.fori_loop(0, part // strip, body, 0, unroll=9)
    write_exps(out_state, 0, exps)
    if members:
        for ref in targets:
            write_exps(ref, part, exps)
    if members == 1:
        out_own[rows + PACK :, :] = asked_ref[...]
    elif not members and has_own:
        out_own[rows:, :] = asked_ref[...]
    elif not members:
        out_own[rows : rows + extra, :] = asked_ref[...]
        out_own[rows + extra :, :] = arrived[1][rows + PACK :, :]


def combine(me, table, levels, rows, own, arrived, bit, members, strip, asked):
    tiles = table.shape[1]
    width_tiles = int(round(((8 * tiles + 1) ** 0.5 - 1) / 2))
    width = width_tiles * LANES
    part = rows // max(members, 1)
    short = jnp.int16
    state = jax.ShapeDtypeStruct((PACK, LANES), short)
    if members > 1:
        message = jax.ShapeDtypeStruct((part + PACK, LANES), short)
        outs = [jax.ShapeDtypeStruct((part, LANES), F32), state] + [message] * (members - 1)
        more = []
    else:
        extra = asked.shape[0]
        size = rows + (PACK + extra if members else extra if own else 2 * extra)
        outs = [jax.ShapeDtypeStruct((size, LANES), short), state]
        more = [asked]
    operands = [*own, *arrived, *more]
    return pl.pallas_call(
        functools.partial(
            combine_kernel,
            levels,
            bit,
            members,
            bool(own),
            len(arrived),
            width_tiles,
            strip,
        ),
        in_specs=[SMEM, SMEM] + [VMEM] * len(operands),
        out_specs=[VMEM] * len(outs),
        out_shape=outs,
        scratch_shapes=[
            pltpu.VMEM((len(arrived), width, LANES), F32),
            pltpu.VMEM((len(arrived), width_tiles, LANES), F32),
            pltpu.VMEM((width, LANES), F32),
            pltpu.VMEM((width_tiles, LANES), F32),
        ],
        compiler_params=pltpu.CompilerParams(vmem_limit_bytes=32 << 20),
        cost_estimate=pl.CostEstimate(
            flops=10 * rows * LANES, bytes_accessed=8 * rows * LANES, transcendentals=0
        ),
        name="sum_shares",
    )(me, table, *operands)


def solve_kernel(
    side,
    levels,
    masks,
    count,
    slot_bits,
    me_ref,
    first_ref,
    second_ref,
    state_ref,
    new_rows_ref,
    scale_ref,
    codes_hbm,
    scores_hbm,
    new_scores_ref,
    flat,
    system,
    pair,
    stored,
    solved,
    columns,
    rows_ref,
    codes,
    scores,
    taken_ref,
    sems,
    out_sems,
):
    lots = sems.shape[0]
    lot = codes.shape[0] // lots

    def fetch(c):
        at = pl.ds(pl.multiple_of(c * lot, lot), lot)
        return pltpu.make_async_copy(codes_hbm.at[at, :], codes.at[at, :], sems.at[c])

    for c in range(lots):
        fetch(c).start()
    queries, width = solved.shape
    tiles = width // LANES
    pieces = len(masks)
    piece = flat.shape[0] // pieces
    pitch = 2 * first_ref.shape[0] // pieces
    asked = []
    for p in range(pieces):
        source = first_ref if p < pieces // 2 else second_ref
        at = p % (pieces // 2) * pitch
        place = pl.multiple_of(offset_of(me_ref[0] ^ masks[p], levels), PACK)
        flat[pl.ds(place, piece), :] = source[at : at + piece, :]
        asked.append(source[at + piece : at + pitch, :].astype(jnp.int32))
    asked = float_of(jnp.concatenate(asked, axis=0)).astype(BF16)
    each = queries // count
    packet = each * tiles
    order = (tiles * queries, asked.shape[0])
    to = lax.broadcasted_iota(jnp.int32, order, 0)
    source = lax.broadcasted_iota(jnp.int32, order, 1)
    slot = lax.shift_right_logical(source, packet.bit_length() - 1)
    owner = jnp.zeros(order, jnp.int32)
    for bit, position in enumerate(slot_bits):
        owner = owner | ((lax.shift_right_logical(slot, position) & 1) << bit)
    owner = owner ^ me_ref[0]
    inside = source & (packet - 1)
    target = (
        lax.shift_right_logical(inside, each.bit_length() - 1) * queries
        + owner * each
        + (inside & (each - 1))
    )
    asked = mm((target == to).astype(F32).astype(BF16), asked)
    for i in range(tiles):
        system[width:, i * LANES : (i + 1) * LANES] = asked[i * queries : (i + 1) * queries, :]
    fill_scales(read_exps(state_ref, 0, tiles), 1.0 / CODE_MAX, columns, rows_ref)
    diagonal = eye(LANES)
    trace = jnp.zeros((1, LANES), F32)
    for b, (i, j) in enumerate(triangle(width)):
        value = flat[b * LANES : (b + 1) * LANES, :].astype(jnp.int32).astype(F32)
        value = value * columns[i * LANES : (i + 1) * LANES, :] * rows_ref[j : j + 1, :]
        system[i * LANES : (i + 1) * LANES, j * LANES : (j + 1) * LANES] = value
        if i == j:
            trace = trace + jnp.sum(jnp.where(diagonal, value, 0.0), axis=0, keepdims=True)
        elif i * LANES // side == j * LANES // side:
            system[j * LANES : (j + 1) * LANES, i * LANES : (i + 1) * LANES] = value.T
    damp = (0.1 / width) * jnp.sum(trace)
    for i in range(tiles):
        at = slice(i * LANES, (i + 1) * LANES)
        system[at, at] += jnp.where(diagonal, damp, 0.0)
    blocks = width // side
    spans = [slice(b * side, (b + 1) * side) for b in range(blocks)]
    unit = eye(side)
    def await_lot(c):
        @pl.when(c < lots)
        def _():
            fetch(c).wait()

    def decode_lot(c):
        start = pl.multiple_of(jnp.minimum(c, lots - 1) * lot, lot)
        decode(codes, scale_ref, start, stored.at[pl.ds(start, lot), :])

    def eliminate(split, mul, refine):
        for b, span in enumerate(spans):
            below = (b + 1) * side
            block = system[span, span]
            bound = jnp.max(jnp.sum(jnp.abs(block), axis=0, keepdims=True))
            low = damp / bound

            def step_from(value, low):
                gain = 4.0 / ((1.0 + low) * (1.0 + low))
                return gain, jnp.where(unit, gain * (1.0 + low), 0.0) - gain * value

            block = block * (1.0 / bound)
            gain, step = step_from(block, low)
            pair[:side, :] = step * (1.0 / bound)
            pair[side:, :] = mul(split(block), split(step))

            def more(low):
                return low < 0.95

            def newton(low):
                taken = taken_ref[0]
                taken_ref[0] = taken + 1
                await_lot(taken)
                both = pair[...]
                gain, step = step_from(both[side:, :], low)
                decode_lot(taken)
                pair[...] = mul(split(both), split(step))
                return gain * low

            low = lax.while_loop(more, newton, gain * low)
            both = pair[...]
            gain, step = step_from(both[side:, :], low)
            low = gain * low
            inverse = mul(split(both[:side, :]), split(step)) * (2.0 / (1.0 + low))
            if refine:
                left = jnp.where(unit, 1.0, 0.0) - mul(split(system[span, span]), split(inverse))
                inverse = inverse + mul(split(inverse), split(left))
            inverse = split(inverse)
            panel = system[below:, span]
            weights = split(mul(split(panel), inverse))
            later = split(panel[: width - below, :])
            system[below:, span] = sum(part.astype(F32) for part in weights)
            for c in range(b + 1, blocks):
                from_row = c * side - below
                update = mul(
                    tuple(part[from_row:, :] for part in weights),
                    tuple(part[from_row : from_row + side, :] for part in later),
                    NT,
                )
                system[c * side :, spans[c]] -= update
        for b in reversed(range(blocks)):
            below = (b + 1) * side
            value = system[width:, spans[b]]
            if below < width:
                value = value - mul(
                    split(solved[:, below:]), split(system[below:width, spans[b]])
                )
            solved[:, spans[b]] = value

    taken_ref[0] = 0
    sums = [jnp.sum(jnp.abs(system[span, span]), axis=0, keepdims=True) for span in spans]
    worst = jnp.max(functools.reduce(jnp.maximum, sums))
    mild = worst <= 800.0 * damp
    pl.when(mild)(lambda: eliminate(split2, mm3, False))
    pl.when(jnp.logical_not(mild))(lambda: eliminate(split3, mm6, True))
    high, low = split2(solved[...])
    new_scores_ref[...] = mm3(split2(new_rows_ref[...]), (high, low), NT)
    both = jnp.concatenate([high, low], axis=0)

    def rest(c, _):
        fetch(c).wait()
        decode_lot(c)
        return 0

    lax.fori_loop(jnp.minimum(taken_ref[0], lots), lots, rest, 0)
    span = scores.shape[1] // out_sems.shape[0]
    copies = []
    for c in range(out_sems.shape[0]):
        at = slice(c * span, (c + 1) * span)
        value = mm(both, stored[at, :], NT)
        scores[:, at] = value[:queries, :] + value[queries:, :]
        out = pltpu.make_async_copy(scores.at[:, at], scores_hbm.at[:, at], out_sems.at[c])
        out.start()
        copies.append(out)
    for out in copies:
        out.wait()


def solve(
    me, levels, masks, count, slot_bits, first, second, state, new_rows, scale_index, codes, asked
):
    rows, width = codes.shape
    examples = new_rows.shape[0]
    side = 256
    flat_rows = len(triangle(width)) * LANES
    return pl.pallas_call(
        functools.partial(solve_kernel, side, levels, masks, count, slot_bits),
        in_specs=[SMEM] + [VMEM] * 5 + [ANY],
        out_specs=[ANY, VMEM],
        out_shape=[
            jax.ShapeDtypeStruct((asked, rows), F32),
            jax.ShapeDtypeStruct((examples, asked), F32),
        ],
        scratch_shapes=[
            pltpu.VMEM((flat_rows, LANES), jnp.int16),
            pltpu.VMEM((width + asked, width), F32),
            pltpu.VMEM((2 * side, side), F32),
            pltpu.VMEM((rows, width), BF16),
            pltpu.VMEM((asked, width), F32),
            pltpu.VMEM((width, LANES), F32),
            pltpu.VMEM((width // LANES, LANES), F32),
            pltpu.VMEM((rows, width), jnp.int32),
            pltpu.VMEM((asked, rows), F32),
            pltpu.SMEM((1,), jnp.int32),
            pltpu.SemaphoreType.DMA((rows // (2 * LANES),)),
            pltpu.SemaphoreType.DMA((8,)),
        ],
        compiler_params=pltpu.CompilerParams(vmem_limit_bytes=46 << 20),
        cost_estimate=pl.CostEstimate(
            flops=10 * 10**9, bytes_accessed=20 * 10**6, transcendentals=0
        ),
        name="solve_and_score",
    )(me, first, second, state, new_rows, scale_index, codes)


def swap(value, mask, count):
    return lax.ppermute(value, "store", [(i, i ^ mask) for i in range(count)])


def shards(activations, out_grads, basis_in, basis_out, lengths, codes, scale_index, queries):
    count = lax.axis_size("store")
    me = lax.axis_index("store").astype(jnp.int32)[None]
    width = codes.shape[1]
    tiles = triangle(width)
    table = np.array(tiles, np.int32).T
    scale_index = scale_index.reshape(-1, LANES)
    new_rows, own, send, state, asked = gram(
        me,
        lengths,
        codes,
        scale_index,
        queries,
        activations,
        out_grads,
        basis_in,
        basis_out,
        count,
    )
    groups = []
    bit = 1
    while 1 << bit < count:
        members = 4 if 1 << (bit + 1) < count else 2
        groups.append((bit, members))
        bit += 2
    piece = len(tiles) * LANES // 2
    for _, members in groups:
        piece //= members if members > 2 else 1
    strip = int(np.gcd(np.gcd(piece, LANES), 64))
    arrived = [swap(send, 1, count)]
    rows = own.shape[0]
    levels = [(0, 2, rows)]
    own = fetch_rows(own, state)
    for bit, members in groups:
        if members == 2:
            coded, _ = combine(me, table, levels, rows, own, arrived, bit, 1, strip, asked)
            own, arrived = [], [coded, swap(coded, 1 << bit, count)]
            break
        own = combine(me, table, levels, rows, own, arrived, bit, members, strip, asked)
        own, messages = own[:2], own[2:]
        arrived = [swap(message, (m + 1) << bit, count) for m, message in enumerate(messages)]
        rows //= members
        levels = levels + [(bit, members, rows)]
    final, state = combine(me, table, levels, rows, own, arrived, 0, 0, strip, asked)
    for bit, members in reversed(groups):
        if members > 2:
            final = jnp.concatenate(
                [final] + [swap(final, m << bit, count) for m in range(1, members)], axis=0
            )
    other = swap(final, 1, count)
    slot_bits = [count.bit_length() - 2]
    for bit, members in groups:
        for low in range(members // 2):
            slot_bits.append(slot_bits[0] - (bit + members // 2 - 1) + low)
    packets = len(tiles) * LANES // rows
    masks = []
    for slot in range(packets):
        first = slot * (count // packets)
        masks.append(sum((first >> position & 1) << b for b, position in enumerate(slot_bits)))
    scores, new_scores = solve(
        me,
        levels,
        masks,
        count,
        slot_bits,
        final,
        other,
        state,
        new_rows,
        scale_index,
        codes,
        count * queries.shape[0],
    )
    return new_rows, scores, new_scores.T


def solution(mesh):
    return jax.shard_map(
        shards,
        mesh=mesh,
        in_specs=(
            P(("groups", "store"), None),
            P(("groups", "store"), None),
            P(),
            P(),
            P(("groups", "store"), None),
            P(("groups", "store"), None),
            P(("groups", "store")),
            P(("groups", "store"), None),
        ),
        out_specs=(P(("groups", "store"), None), P("groups", "store"), P("groups", "store")),
        check_vma=False,
    )
```
